128 devices in a mesh: row: 16 (over y, x), col: 8 (over z, core).
Axes of the slice: x: 4, y: 4, z: 4, core: 2. Of those that a mesh axis runs over, the one named last changes fastest.
Arguments:
- audio: float32 [16384, 768], P(('row', 'col')), may hold values from -80 to 80, as said below
- video: float32 [16384, 768], P(('col', 'row')), may hold values from -80 to 80, as said below
Outputs:
- loss: float32 [], replicated
- audio_grad: float32 [16384, 768], P(('row', 'col'))
- video_grad: float32 [16384, 768], P(('col', 'row'))
The draws below stay inside these ranges and needn't reach their ends.
Inputs may be any that keep to these rules, and one draw needn't show every extreme that they name: audio embeddings, float32. video embeddings, float32.
All inputs are finite; a program needn't handle non-finite values.
Results may differ from the reference program's by a relative error of at most 0.0014.
Values sent between devices are 32-bit elements; how exact they have to be, the bound alone decides.
No kernel may reach another device: no remote copies, remote signals or barrier semaphores. Data moves between devices by JAX's collectives and lax.ppermute only.
A program may use at most 128 MiB of HBM per device.

```python
import jax
import jax.numpy as jnp
from jax import lax

D = 768
ITERS = 3
CLIPS = 16384


def shared_content(key):
    return jnp.clip(jax.random.normal(key, (CLIPS, D), jnp.float32), -4.0, 4.0)


def tower_view(key, salt):
    common = shared_content(key)
    key = jax.random.fold_in(key, salt)
    noise_key = jax.random.fold_in(key, 0)
    noise = jnp.clip(jax.random.normal(noise_key, (CLIPS, D), jnp.float32), -4.0, 4.0)
    return common + noise


def draw_audio(key, part):
    return tower_view(key, 11)


def draw_video(key, part):
    return tower_view(key, 23)


def setup_inputs(seed: int = 0) -> dict:
    key_list = jax.random.split(jax.random.key(seed), 3)
    return {
        "audio": draw_audio(jax.random.fold_in(key_list[2], 71), 0),
        "video": draw_video(jax.random.fold_in(key_list[2], 71), 0),
    }


HIGH = lax.Precision.HIGHEST

def unit_rows(values):
    inv = lax.rsqrt(lax.optimization_barrier(jnp.sum(values * values, axis=1, keepdims=True)) + 1e-06)
    return (values * inv, inv)

def reference(audio, video):
    audio_unit, audio_inv = unit_rows(audio)
    video_unit, video_inv = unit_rows(video)
    scores = 20.0 * jnp.dot(audio_unit, video_unit.T, precision=HIGH, preferred_element_type=jnp.float32)
    kernel = jnp.exp(scores)
    col_scale = jnp.ones((kernel.shape[1],), jnp.float32)
    row_scale = jnp.ones((kernel.shape[0],), jnp.float32)
    for step in range(ITERS):
        row_scale = 1.0 / lax.optimization_barrier(jnp.sum(kernel * col_scale[None, :], axis=1))
        col_scale = 1.0 / lax.optimization_barrier(jnp.sum(kernel * row_scale[:, None], axis=0))
    target = kernel * row_scale[:, None] * col_scale[None, :]
    target_rows = lax.optimization_barrier(jnp.sum(target, axis=1))
    totals = lax.optimization_barrier(jnp.sum(kernel, axis=1))
    count = kernel.shape[0]
    loss = -jnp.sum(target * (scores - jnp.log(totals)[:, None])) / count
    score_grad = ((target_rows / totals)[:, None] * kernel - target) / count
    unit_audio = 20.0 * jnp.dot(score_grad, video_unit, precision=HIGH, preferred_element_type=jnp.float32)
    unit_video = 20.0 * jnp.dot(score_grad.T, audio_unit, precision=HIGH, preferred_element_type=jnp.float32)
    audio_grad = (unit_audio - audio_unit * lax.optimization_barrier(jnp.sum(audio_unit * unit_audio, axis=1, keepdims=True))) * audio_inv
    video_grad = (unit_video - video_unit * lax.optimization_barrier(jnp.sum(video_unit * unit_video, axis=1, keepdims=True))) * video_inv
    return (loss, audio_grad, video_grad)
```

```python
import jax
import jax.numpy as jnp
from jax import lax
from jax.experimental import pallas as pl
from jax.experimental.pallas import tpu as pltpu
from jax.sharding import PartitionSpec as P

ITERS = 3
F32 = jnp.float32
BF16 = jnp.bfloat16
VMEM_BYTES = 56 * 1024 * 1024
ORDER = (0, -1, 1, 2)


def params(limit=VMEM_BYTES, **kw):
    return pltpu.CompilerParams(vmem_limit_bytes=limit, **kw)


def vmem():
    return pl.BlockSpec(memory_space=pltpu.VMEM)


def smem():
    return pl.BlockSpec(memory_space=pltpu.SMEM)


def split(value):
    high = value.astype(BF16)
    return high, (value - high.astype(F32)).astype(BF16)


def dot3(lhs, rhs, dims):
    (lh, ll), (rh, rl) = lhs, rhs
    dot = lambda p, q: lax.dot_general(p, q, (dims, ((), ())), preferred_element_type=F32)
    return dot(lh, rh) + (dot(lh, rl) + dot(ll, rh))


def unit_kernel(a_ref, v_ref, au_ref, vu_ref, ai_ref, vi_ref):
    for src, dst, inv_ref in ((a_ref, au_ref, ai_ref), (v_ref, vu_ref, vi_ref)):
        x = src[...]
        inv = lax.rsqrt(jnp.sum(x * x, axis=1, keepdims=True) + 1e-06)
        dst[...] = x * inv
        inv_ref[...] = jnp.broadcast_to(inv, inv_ref.shape)


def unit_rows(audio, video):
    n, d = audio.shape
    return pl.pallas_call(
        unit_kernel,
        out_shape=[jax.ShapeDtypeStruct((n, d), F32)] * 2 + [jax.ShapeDtypeStruct((n, 128), F32)] * 2,
        in_specs=[vmem()] * 2,
        out_specs=[vmem()] * 4,
        compiler_params=params(),
        name="unit_rows",
    )(audio, video)


def scores_kernel(pos_ref, a_ref, *refs):
    pieces, (kt_ref, ah_ref, al_ref, vh_ref, vl_ref, sum_ref) = refs[:8], refs[8:]
    ah, al = split(a_ref[...])
    ah_ref[...] = ah
    al_ref[...] = al
    total = jnp.zeros((8, a_ref.shape[0]), F32)
    for p, piece in enumerate(pieces):
        vh, vl = split(piece[...])
        s = dot3((vh, vl), (ah_ref[...], al_ref[...]), ((1,), (1,)))
        k = jnp.exp(20.0 * s)
        total = total + jnp.sum(k.reshape(32, 8, -1), axis=0)
        half, j = p // 4, p % 4
        major = (pos_ref[half] + ORDER[j] + 4) % 4
        for b in range(4):
            minor = (pos_ref[1 - half] + ORDER[b] + 4) % 4
            at = pl.ds(pl.multiple_of(half * 1024 + major * 256 + minor * 64, 64), 64)
            rows = slice(b * 64, b * 64 + 64)
            kt_ref[at, :] = k[rows]
            vh_ref[at, :] = vh[rows]
            vl_ref[at, :] = vl[rows]
    put_lanes(sum_ref, jnp.sum(total, axis=0, keepdims=True))


def put_lanes(ref, row):
    copies, chunks, _ = ref.shape
    for m in range(chunks):
        part = row[:, m * 128 : m * 128 + 128]
        for d in range(copies):
            ref[d, m : m + 1, :] = part


def scores(pos, audio_tile, pieces):
    n, d = audio_tile.shape
    m = 2048
    return pl.pallas_call(
        scores_kernel,
        out_shape=[
            jax.ShapeDtypeStruct((m, n), F32),
            jax.ShapeDtypeStruct((n, d), BF16),
            jax.ShapeDtypeStruct((n, d), BF16),
            jax.ShapeDtypeStruct((m, d), BF16),
            jax.ShapeDtypeStruct((m, d), BF16),
            jax.ShapeDtypeStruct((8, 8, 128), F32),
        ],
        in_specs=[smem()] + [vmem()] * 9,
        out_specs=[vmem()] * 6,
        compiler_params=params(),
        name="scores",
    )(pos, audio_tile, *pieces)


def scale_of(part_ref):
    return 1.0 / jnp.sum(part_ref[...], axis=0)


def columns_kernel(part_ref, kt_ref, out_ref):
    r = scale_of(part_ref)
    k = pl.program_id(0)
    for b in range(2):
        acc = jnp.zeros((128, 128), F32)
        for m in range(8):
            acc = acc + kt_ref[b * 128 : b * 128 + 128, m * 128 : m * 128 + 128] * r[m : m + 1, :]
        row = jnp.sum(acc.T, axis=0, keepdims=True)
        for d in range(16):
            out_ref[d, pl.ds(k * 2 + b, 1), :] = row


def rows_kernel(part_ref, kt_ref, out_ref, scale_ref, acc_ref):
    k = pl.program_id(0)

    @pl.when(k == 0)
    def _():
        scale_ref[...] = scale_of(part_ref)
        acc_ref[...] = jnp.zeros_like(acc_ref)

    for b in range(2):
        c = jnp.broadcast_to(scale_ref[pl.ds(k * 2 + b, 1), :], (128, 128)).T
        for m in range(8):
            lanes = slice(m * 128, m * 128 + 128)
            prod = kt_ref[b * 128 : b * 128 + 128, lanes] * c
            acc_ref[:, lanes] += jnp.sum(prod.reshape(16, 8, 128), axis=0)

    @pl.when(k == 7)
    def _():
        put_lanes(out_ref, jnp.sum(acc_ref[...], axis=0, keepdims=True))


def whole(shape):
    return pl.BlockSpec(shape, lambda k: (0,) * len(shape))


def columns_pass(part, kt):
    return pl.pallas_call(
        columns_kernel,
        grid=(8,),
        out_shape=jax.ShapeDtypeStruct((16, 16, 128), F32),
        in_specs=[whole((8, 8, 128)), pl.BlockSpec((256, 1024), lambda k: (k, 0))],
        out_specs=whole((16, 16, 128)),
        compiler_params=params(),
        name="column_sums",
    )(part, kt)


def rows_pass(part, kt):
    return pl.pallas_call(
        rows_kernel,
        grid=(8,),
        out_shape=jax.ShapeDtypeStruct((8, 8, 128), F32),
        in_specs=[whole((16, 16, 128)), pl.BlockSpec((256, 1024), lambda k: (k, 0))],
        out_specs=whole((8, 8, 128)),
        scratch_shapes=[pltpu.VMEM((16, 128), F32), pltpu.VMEM((8, 1024), F32)],
        compiler_params=params(),
        name="row_sums",
    )(part, kt)


def grads_kernel(count, tot_ref, rp_ref, cp_ref, tp_ref, kt_ref, ah_ref, al_ref, vh_ref, vl_ref,
                 y_ref, u_ref, loss_ref, c_ref, r_ref, w_ref, log_ref):
    k = pl.program_id(0)

    @pl.when(k == 0)
    def _():
        c_ref[...] = scale_of(cp_ref)
        totals = jnp.sum(tot_ref[...], axis=0)
        r = scale_of(rp_ref)
        w = r * jnp.sum(tp_ref[...], axis=0) / totals
        logs = jnp.log(totals)
        for m in range(8):
            lanes = slice(m * 128, m * 128 + 128)
            r_ref[:, lanes] = jnp.broadcast_to(r[m : m + 1], (8, 128))
            w_ref[:, lanes] = jnp.broadcast_to(w[m : m + 1], (8, 128))
            log_ref[:, lanes] = jnp.broadcast_to(logs[m : m + 1], (8, 128))
        u_ref[...] = jnp.zeros_like(u_ref)
        loss_ref[...] = jnp.zeros_like(loss_ref)

    c = jnp.concatenate(
        [jnp.broadcast_to(c_ref[pl.ds(k * 2 + b, 1), :], (128, 128)).T for b in range(2)], axis=0
    )
    c = jnp.concatenate([c] * 8, axis=1)
    kernel = kt_ref[...]
    scaled = r_ref[0:1, :] * c
    g = kernel * ((w_ref[0:1, :] - scaled) * (20.0 / count))
    terms = kernel * scaled * (jnp.log(kernel) - log_ref[0:1, :])
    terms = jnp.sum(terms.reshape(32, 8, 1024), axis=0)
    loss_ref[...] += sum(terms[:, m * 128 : m * 128 + 128] for m in range(8))
    g = split(g)
    y_ref[...] = dot3(g, (ah_ref[...], al_ref[...]), ((1,), (0,)))
    u_ref[...] += dot3(g, (vh_ref[...], vl_ref[...]), ((0,), (0,)))


def grads(count, tot, rpart, cpart, tpart, kt, ah, al, vh, vl):
    vec = whole((8, 8, 128))
    return pl.pallas_call(
        lambda *refs: grads_kernel(count, *refs),
        grid=(8,),
        out_shape=[
            jax.ShapeDtypeStruct((2048, 768), F32),
            jax.ShapeDtypeStruct((1024, 768), F32),
            jax.ShapeDtypeStruct((8, 128), F32),
        ],
        in_specs=[
            vec, vec, whole((16, 16, 128)), vec,
            pl.BlockSpec((256, 1024), lambda k: (k, 0)),
            whole((1024, 768)), whole((1024, 768)),
            pl.BlockSpec((256, 768), lambda k: (k, 0)),
            pl.BlockSpec((256, 768), lambda k: (k, 0)),
        ],
        out_specs=[
            pl.BlockSpec((256, 768), lambda k: (k, 0)),
            whole((1024, 768)),
            whole((8, 128)),
        ],
        scratch_shapes=[pltpu.VMEM((16, 128), F32)] + [pltpu.VMEM((8, 1024), F32)] * 3,
        compiler_params=params(),
        name="unit_grads",
    )(tot, rpart, cpart, tpart, kt, ah, al, vh, vl)


def step_y(v, k):
    return lax.ppermute(v, "row", [(i, ((i // 4 + k) % 4) * 4 + i % 4) for i in range(16)])


def step_x(v, k):
    return lax.ppermute(v, "row", [(i, (i // 4) * 4 + (i % 4 + k) % 4) for i in range(16)])


def ring_gather(step, v):
    half = v.shape[0] // 2
    left, right = step(v, 1), step(v, -1)
    far = jnp.concatenate([step(left[:half], 1), step(right[half:], -1)], axis=0)
    return [v, left, right, far]


def gather_video(v):
    half = v.shape[0] // 2
    first = jnp.concatenate(ring_gather(step_x, v[:half]), axis=0)
    second = jnp.concatenate(ring_gather(step_y, v[half:]), axis=0)
    return ring_gather(step_y, first) + ring_gather(step_x, second)


def ring_scatter(step, v, me):
    size = v.shape[0] // 4
    half = size // 2
    block = lambda k: lax.dynamic_slice_in_dim(v, ((me + k) % 4) * size, size, 0)
    far = block(2)
    from_left, from_right = step(far[:half], 1), step(far[half:], -1)
    up, down = block(1), block(3)
    up = jnp.concatenate([up[:half] + from_left, up[half:]], axis=0)
    down = jnp.concatenate([down[:half], down[half:] + from_right], axis=0)
    return block(0) + step(up, 1) + step(down, -1)


def scatter_video(v, y, x):
    half = v.shape[0] // 2
    first = ring_scatter(step_x, ring_scatter(step_y, v[:half], y), x)
    second = ring_scatter(step_y, ring_scatter(step_x, v[half:], x), y)
    return jnp.concatenate([first, second], axis=0)


def swap(part, axis):
    return lax.all_to_all(part, axis, 0, 0, tiled=True)


def local(audio, video):
    count = audio.shape[0] * 128
    row = lax.axis_index("row")
    y, x = row // 4, row % 4
    pos = jnp.stack([y, x]).astype(jnp.int32)
    audio_unit, video_unit, audio_inv, video_inv = unit_rows(audio, video)
    audio_tile = lax.all_gather(audio_unit, "col", axis=0, tiled=True)
    pieces = gather_video(video_unit)
    kt, ah, al, vh, vl, part = scores(pos, audio_tile, pieces)
    totals = swap(part, "col")
    rpart = totals
    for step in range(ITERS):
        cpart = swap(columns_pass(rpart, kt), "row")
        part = swap(rows_pass(cpart, kt), "col")
        if step < ITERS - 1:
            rpart = part
    full_video, full_audio, terms = grads(count, totals, rpart, cpart, part, kt, ah, al, vh, vl)
    terms = jnp.sum(swap(jnp.broadcast_to(terms[None], (8, 8, 128)), "col"), axis=0)
    terms = swap(jnp.broadcast_to(terms[None], (16, 8, 128)), "row")
    loss = -jnp.sum(terms) / count
    unit_audio = lax.psum_scatter(full_audio, "col", scatter_dimension=0, tiled=True)
    unit_video = scatter_video(full_video, y, x)

    def project(unit, grad, inv):
        return (grad - unit * jnp.sum(unit * grad, axis=1, keepdims=True)) * inv[:, :1]

    return (
        loss,
        project(audio_unit, unit_audio, audio_inv),
        project(video_unit, unit_video, video_inv),
    )


def solution(mesh):
    in_specs = (P(("row", "col"), None), P(("col", "row"), None))
    out_specs = (P(), P(("row", "col"), None), P(("col", "row"), None))
    return jax.shard_map(local, mesh=mesh, in_specs=in_specs, out_specs=out_specs, check_vma=False)
```

```python
import jax
import jax.numpy as jnp
from jax import lax
from jax.experimental import pallas as pl
from jax.experimental.pallas import tpu as pltpu
from jax.sharding import PartitionSpec as P

ITERS = 3
F32 = jnp.float32
BF16 = jnp.bfloat16
MIB = 1024 * 1024
NEAR = (0, -1, 1, 2)


def vmem():
    return pl.BlockSpec(memory_space=pltpu.VMEM)


def smem():
    return pl.BlockSpec(memory_space=pltpu.SMEM)


def f32(*shape):
    return jax.ShapeDtypeStruct(shape, F32)


def bf16(*shape):
    return jax.ShapeDtypeStruct(shape, BF16)


def call(kernel, name, outs, *args, pos=None, scratch=(), mib=7, flops=0):
    specs = [vmem()] * len(args)
    if pos is not None:
        specs, args = [smem()] + specs, (pos,) + args
    size = lambda arrays: sum(a.size * a.dtype.itemsize for a in arrays)
    return pl.pallas_call(
        kernel,
        out_shape=list(outs),
        in_specs=specs,
        out_specs=[vmem()] * len(outs),
        scratch_shapes=list(scratch),
        compiler_params=pltpu.CompilerParams(vmem_limit_bytes=mib * MIB),
        cost_estimate=pl.CostEstimate(
            flops=flops, bytes_accessed=size(args) + size(outs), transcendentals=0
        ),
        name=name,
    )(*args)


def split(value):
    high = value.astype(BF16)
    return high, (value - high.astype(F32)).astype(BF16)


def dot3(lhs, rhs, dims):
    (lh, ll), (rh, rl) = lhs, rhs
    dot = lambda p, q: lax.dot_general(p, q, (dims, ((), ())), preferred_element_type=F32)
    return dot(lh, rh) + (dot(lh, rl) + dot(ll, rh))


def inverse_length(x):
    return lax.rsqrt(jnp.sum(x * x, axis=1, keepdims=True) + 1e-06)


def unit_kernel(a_ref, v_ref, au_ref, vt_ref, vb_ref):
    a = a_ref[...]
    au_ref[...] = a * inverse_length(a)
    v = v_ref[...]
    v = v * inverse_length(v)
    vt_ref[...] = v[:64]
    vb_ref[...] = v[64:]


LAYOUT = (
    ((0, 0), (1, 0)),
    ((0, 1), (0, 2), (1, 1), (1, 2)),
    ((0, 3), (1, 3)),
)


def join_kernel(half, pos_ref, own, left, right, far, out_ref):
    for j, ref in enumerate((own, left, right, far)):
        at = ((pos_ref[1 - half] + NEAR[j] + 4) % 4) * 64
        out_ref[pl.ds(pl.multiple_of(at, 64), 64), :] = ref[...]


def halves_kernel(left, right, a_ref, b_ref):
    a_ref[...] = left[0:128, :]
    b_ref[...] = right[128:256, :]


def pieces_body(total, pieces, ah_ref, al_ref, k_ref, vh_ref, vl_ref):
    at = 0
    for piece in pieces:
        rows = slice(at, at + piece.shape[0])
        vh_ref[rows, :], vl_ref[rows, :] = split(piece[...])
        at += piece.shape[0]
        if at % 256 == 0:
            rows = slice(at - 256, at)
            video = (vh_ref[rows, :], vl_ref[rows, :])
            k = jnp.exp(20.0 * dot3(video, (ah_ref[...], al_ref[...]), ((1,), (1,))))
            k_ref[rows, :] = k
            total = total + jnp.sum(k.reshape(-1, 8, k.shape[1]), axis=0)
    return total


def scores_own_kernel(a_ref, p_ref, q_ref, ah_ref, al_ref, k_ref, vh_ref, vl_ref, sum_ref):
    ah_ref[...], al_ref[...] = split(a_ref[...])
    sum_ref[...] = pieces_body(0.0, (p_ref, q_ref), ah_ref, al_ref, k_ref, vh_ref, vl_ref)


def scores_near_kernel(ah_ref, al_ref, in_ref, p0, p1, p2, p3, k_ref, vh_ref, vl_ref, sum_ref):
    sum_ref[...] = pieces_body(in_ref[...], (p0, p1, p2, p3), ah_ref, al_ref, k_ref, vh_ref, vl_ref)


def scores_far_kernel(ah_ref, al_ref, in_ref, p0, p1, q0, q1, k_ref, vh_ref, vl_ref, sum_ref):
    total = pieces_body(in_ref[...], (p0, p1, q0, q1), ah_ref, al_ref, k_ref, vh_ref, vl_ref)
    put_lanes(sum_ref, jnp.sum(total, axis=0, keepdims=True))


def put_lanes(ref, row):
    for m in range(8):
        part = row[:, m * 128 : m * 128 + 128]
        for d in range(8):
            ref[d, m : m + 1, :] = part


def scale_of(part_ref):
    return 1.0 / jnp.sum(part_ref[...], axis=0)


def chunk_of(pos_ref, half, j, b):
    return half * 8 + ((pos_ref[half] + NEAR[j] + 4) % 4) * 2 + b


def chunks(pos_ref, k_refs):
    for ref, blocks in zip(k_refs, LAYOUT):
        for n, (half, j) in enumerate(blocks):
            for b in range(2):
                yield ref, n * 256 + b * 128, chunk_of(pos_ref, half, j, b)


def down(scale_ref, chunk):
    return jnp.broadcast_to(scale_ref[pl.ds(chunk, 1), :], (128, 128)).T


def columns_kernel(pos_ref, part_ref, k1_ref, k2_ref, k3_ref, out_ref):
    r = scale_of(part_ref)
    for ref, at, chunk in chunks(pos_ref, (k1_ref, k2_ref, k3_ref)):
        acc = ref[at : at + 128, 0:128] * r[0:1, :]
        for m in range(1, 8):
            acc = acc + ref[at : at + 128, m * 128 : m * 128 + 128] * r[m : m + 1, :]
        row = jnp.sum(acc.T, axis=0, keepdims=True)
        for d in range(16):
            out_ref[d, pl.ds(chunk, 1), :] = row


def fold(value):
    return jnp.sum(value.reshape(16, 8, 128), axis=0)


def rows_kernel(pos_ref, part_ref, k1_ref, k2_ref, k3_ref, out_ref, scale_ref):
    scale_ref[...] = scale_of(part_ref)
    acc = [0.0] * 8
    for ref, at, chunk in chunks(pos_ref, (k1_ref, k2_ref, k3_ref)):
        c = down(scale_ref, chunk)
        for m in range(8):
            acc[m] = acc[m] + fold(ref[at : at + 128, m * 128 : m * 128 + 128] * c)
    put_lanes(out_ref, jnp.concatenate([jnp.sum(a, axis=0, keepdims=True) for a in acc], axis=1))


def last_rows_kernel(pos_ref, part_ref, rpart_ref, tot_ref, k1_ref, k2_ref, k3_ref, out_ref, scale_ref):
    scale_ref[...] = scale_of(part_ref)
    acc, weighted = [0.0] * 8, [0.0] * 8
    for ref, at, chunk in chunks(pos_ref, (k1_ref, k2_ref, k3_ref)):
        c = down(scale_ref, chunk)
        for m in range(8):
            kernel = ref[at : at + 128, m * 128 : m * 128 + 128]
            prod = kernel * c
            acc[m] = acc[m] + fold(prod)
            weighted[m] = weighted[m] + fold(prod * jnp.log(kernel))
    r = scale_of(rpart_ref)
    logs = jnp.log(jnp.sum(tot_ref[...], axis=0))
    terms = sum(r[m : m + 1] * (weighted[m] - logs[m : m + 1] * acc[m]) for m in range(8))
    put_lanes(out_ref, jnp.concatenate([jnp.sum(a, axis=0, keepdims=True) for a in acc], axis=1))
    for d in range(8):
        out_ref[d, 8:16, :] = terms


def grad_scales(count, tot_ref, rp_ref, cp_ref, tp_ref, c_ref, r_ref, w_ref):
    c_ref[...] = scale_of(cp_ref)
    r = scale_of(rp_ref) * (20.0 / count)
    w = r * jnp.sum(tp_ref[:, 0:8, :], axis=0) / jnp.sum(tot_ref[...], axis=0)
    for m in range(8):
        lanes = slice(m * 128, m * 128 + 128)
        r_ref[:, lanes] = jnp.broadcast_to(r[m : m + 1], (8, 128))
        w_ref[:, lanes] = jnp.broadcast_to(w[m : m + 1], (8, 128))


def grad_block(pos_ref, half, j, k_ref, at, c_ref, r_ref, w_ref):
    c = jnp.concatenate([down(c_ref, chunk_of(pos_ref, half, j, b)) for b in range(2)], axis=0)
    c = jnp.concatenate([c] * 8, axis=1)
    return split(k_ref[at : at + 256, :] * (w_ref[0:1, :] - r_ref[0:1, :] * c))


SCALES = [pltpu.VMEM((16, 128), F32), pltpu.VMEM((8, 1024), F32), pltpu.VMEM((8, 1024), F32)]


def far_kernel(count, pos_ref, tot_ref, rp_ref, cp_ref, tp_ref, k_ref, ah_ref, al_ref,
               yu_ref, yd_ref, xu_ref, xd_ref, c_ref, r_ref, w_ref):
    grad_scales(count, tot_ref, rp_ref, cp_ref, tp_ref, c_ref, r_ref, w_ref)
    for half, (u_ref, d_ref) in enumerate(((yu_ref, yd_ref), (xu_ref, xd_ref))):
        g = grad_block(pos_ref, half, 3, k_ref, half * 256, c_ref, r_ref, w_ref)
        out = dot3(g, (ah_ref[...], al_ref[...]), ((1,), (0,)))
        u_ref[0:128, :] = out[:128]
        d_ref[0:128, :] = out[128:]
    terms = jnp.concatenate([jnp.sum(tp_ref[:, 8:16, :], axis=0)] * 6, axis=1)
    yu_ref[128:136, :] = terms
    yd_ref[128:136, :] = terms


def audio_body(pos_ref, layouts, start, u_ref, c_ref, r_ref, w_ref):
    for k_ref, h_ref, l_ref, blocks in layouts:
        for n, (half, j) in enumerate(blocks):
            at = slice(n * 256, n * 256 + 256)
            g = grad_block(pos_ref, half, j, k_ref, n * 256, c_ref, r_ref, w_ref)
            for m in range(4):
                lanes = slice(m * 256, m * 256 + 256)
                part = tuple(v[:, lanes] for v in g)
                out = dot3(part, (h_ref[at, :], l_ref[at, :]), ((0,), (0,)))
                u_ref[lanes, :] = out if start is None else start[lanes, :] + out
            start = u_ref


def audio_first_kernel(count, pos_ref, tot_ref, rp_ref, cp_ref, tp_ref, k1_ref, k3_ref,
                       h1_ref, l1_ref, h3_ref, l3_ref, u_ref, c_ref, r_ref, w_ref):
    grad_scales(count, tot_ref, rp_ref, cp_ref, tp_ref, c_ref, r_ref, w_ref)
    layouts = ((k1_ref, h1_ref, l1_ref, LAYOUT[0]), (k3_ref, h3_ref, l3_ref, LAYOUT[2]))
    audio_body(pos_ref, layouts, None, u_ref, c_ref, r_ref, w_ref)


def audio_second_kernel(count, pos_ref, tot_ref, rp_ref, cp_ref, tp_ref, k2_ref, h2_ref, l2_ref,
                        in_ref, u_ref, c_ref, r_ref, w_ref):
    grad_scales(count, tot_ref, rp_ref, cp_ref, tp_ref, c_ref, r_ref, w_ref)
    audio_body(pos_ref, ((k2_ref, h2_ref, l2_ref, LAYOUT[1]),), in_ref, u_ref, c_ref, r_ref, w_ref)


def near_kernel(count, pos_ref, tot_ref, rp_ref, cp_ref, tp_ref, k_ref, ah_ref, al_ref,
                yl_ref, yr_ref, xl_ref, xr_ref, yu_ref, yd_ref, xu_ref, xd_ref, c_ref, r_ref, w_ref):
    grad_scales(count, tot_ref, rp_ref, cp_ref, tp_ref, c_ref, r_ref, w_ref)
    for n, (ref, left, right) in enumerate((
        (yd_ref, None, yr_ref), (yu_ref, yl_ref, None), (xd_ref, None, xr_ref), (xu_ref, xl_ref, None)
    )):
        half, j = LAYOUT[1][n]
        g = grad_block(pos_ref, half, j, k_ref, n * 256, c_ref, r_ref, w_ref)
        out = dot3(g, (ah_ref[...], al_ref[...]), ((1,), (0,)))
        ref[0:128, :] = out[:128] if left is None else out[:128] + left[0:128, :]
        ref[128:256, :] = out[128:] if right is None else out[128:] + right[0:128, :]
    yu_ref[256:264, :] = yl_ref[128:136, :]


def own_kernel(count, pos_ref, tot_ref, rp_ref, cp_ref, tp_ref, k_ref, ah_ref, al_ref,
               y_ref, x_ref, c_ref, r_ref, w_ref):
    grad_scales(count, tot_ref, rp_ref, cp_ref, tp_ref, c_ref, r_ref, w_ref)
    for half, ref in enumerate((y_ref, x_ref)):
        g = grad_block(pos_ref, half, 0, k_ref, half * 256, c_ref, r_ref, w_ref)
        ref[...] = dot3(g, (ah_ref[...], al_ref[...]), ((1,), (0,)))


def ordered_sum(me, values, order_ref):
    for k, value in enumerate(values):
        order_ref[pl.ds(pl.multiple_of(((me + k) % 4) * 8, 8), 8), :] = value
    return jnp.sum(order_ref[...].reshape(4, 8, 128), axis=0)


def middle_kernel(pos_ref, tp_ref, yl_ref, yr_ref, y_ref, x_ref, yu_ref, yd_ref, xu_ref, xd_ref,
                  y1_ref, y2_ref, y3_ref, y0_ref, x1_ref, x2_ref, x3_ref, x0_ref, sum_ref, order_ref):
    terms = ordered_sum(
        pos_ref[0],
        (jnp.sum(tp_ref[:, 8:16, :], axis=0), yr_ref[128:136, 0:128], yu_ref[256:264, 0:128],
         yl_ref[128:136, 0:128]),
        order_ref,
    )
    for half, (own, up, down, outs) in enumerate((
        (y_ref, yu_ref, yd_ref, (y0_ref, y1_ref, y2_ref, y3_ref)),
        (x_ref, xu_ref, xd_ref, (x0_ref, x1_ref, x2_ref, x3_ref)),
    )):
        sum_ref[...] = own[...] + up[0:256, :] + down[...]
        for k, ref in enumerate(outs):
            at = ((pos_ref[1 - half] + k) % 4) * 64
            ref[0:64, :] = sum_ref[pl.ds(pl.multiple_of(at, 64), 64), :]
            if half == 0:
                ref[64:72, :] = jnp.concatenate([terms] * 6, axis=1)


def project(x, grad):
    inv = inverse_length(x)
    unit = x * inv
    return (grad - unit * jnp.sum(unit * grad, axis=1, keepdims=True)) * inv


def video_kernel(count, pos_ref, v_ref, y0, y1, y2, y3, x0, x1, x2, x3, out_ref, loss_ref, order_ref):
    top = y0[0:64, :] + y1[0:64, :] + y2[0:64, :] + y3[0:64, :]
    bottom = x0[...] + x1[...] + x2[...] + x3[...]
    out_ref[0:64, :] = project(v_ref[0:64, :], top)
    out_ref[64:128, :] = project(v_ref[64:128, :], bottom)
    terms = ordered_sum(
        pos_ref[1], tuple(ref[64:72, 0:128] for ref in (y0, y3, y2, y1)), order_ref
    )
    loss_ref[...] = jnp.full((1, 1), -jnp.sum(terms) / count)


def audio_project_kernel(x_ref, grad_ref, out_ref):
    out_ref[...] = project(x_ref[...], grad_ref[...])


def step_y(v, k):
    return lax.ppermute(v, "row", [(i, ((i // 4 + k) % 4) * 4 + i % 4) for i in range(16)])


def step_x(v, k):
    return lax.ppermute(v, "row", [(i, (i // 4) * 4 + (i % 4 + k) % 4) for i in range(16)])


def swap(part, axis):
    return lax.all_to_all(part, axis, 0, 0, tiled=True)


def local(audio, video):
    count = audio.shape[0] * 128
    bind = lambda kernel: lambda *refs: kernel(count, *refs)
    row = lax.axis_index("row")
    pos = jnp.stack([row // 4, row % 4]).astype(jnp.int32)
    audio_unit, vt, vb = call(
        unit_kernel, "unit_rows", [f32(128, 768), f32(64, 768), f32(64, 768)], audio, video
    )
    audio_tile = lax.all_gather(audio_unit, "col", axis=0, tiled=True)
    join = lambda half, *parts: call(
        lambda *refs: join_kernel(half, *refs), "join", [f32(256, 768)], *parts, pos=pos, mib=4
    )[0]
    xl, xr, yl, yr = step_x(vt, 1), step_x(vt, -1), step_y(vb, 1), step_y(vb, -1)
    first = join(0, vt, xl, xr, step_x(vt, 2))
    second = join(1, vb, yl, yr, step_y(yr, -1))
    fl, fr, sl, sr = step_y(first, 1), step_y(first, -1), step_x(second, 1), step_x(second, -1)
    flops = 3 * 2 * 1024 * 768
    ah, al, k1, h1, l1, sums = call(
        scores_own_kernel, "scores_own",
        [bf16(1024, 768), bf16(1024, 768), f32(512, 1024), bf16(512, 768), bf16(512, 768), f32(8, 1024)],
        audio_tile, first, second, flops=512 * flops,
    )
    fl, fr, sl, sr, sums = lax.optimization_barrier((fl, fr, sl, sr, sums))
    halves = lambda left, right: call(halves_kernel, "halves", [f32(128, 768)] * 2, left, right, mib=4)
    a, b = halves(fl, fr)
    c, d = halves(sl, sr)
    far = (step_y(a, 1), step_y(b, -1), step_x(c, 1), step_x(d, -1))
    k2, h2, l2, sums = call(
        scores_near_kernel, "scores_near",
        [f32(1024, 1024), bf16(1024, 768), bf16(1024, 768), f32(8, 1024)],
        ah, al, sums, fl, fr, sl, sr, flops=1024 * flops,
    )
    k3, h3, l3, part = call(
        scores_far_kernel, "scores_far",
        [f32(512, 1024), bf16(512, 768), bf16(512, 768), f32(8, 8, 128)],
        ah, al, sums, *far, flops=512 * flops,
    )
    ks = (k1, k2, k3)
    scale = pltpu.VMEM((16, 128), F32)
    totals = swap(part, "col")
    rpart = totals
    for step in range(ITERS):
        cpart = swap(call(columns_kernel, "column_sums", [f32(16, 16, 128)], rpart, *ks, pos=pos, mib=9)[0], "row")
        if step < ITERS - 1:
            part = call(rows_kernel, "row_sums", [f32(8, 8, 128)], cpart, *ks, pos=pos, mib=9, scratch=[scale])[0]
            rpart = swap(part, "col")
    part = call(last_rows_kernel, "row_sums_and_loss", [f32(8, 16, 128)], cpart, rpart, totals, *ks,
                pos=pos, mib=9, scratch=[scale])[0]
    tpart = swap(part, "col")

    vectors = (totals, rpart, cpart, tpart)
    block = f32(256, 768)
    yu, yd, xu, xd = call(
        bind(far_kernel), "video_far", [f32(136, 768), f32(136, 768), f32(128, 768), f32(128, 768)],
        *vectors, k3, ah, al, pos=pos, scratch=SCALES, flops=512 * flops,
    )
    after, yu = lax.optimization_barrier((tpart, yu))
    yl, yr, xl, xr = step_y(yu, 1), step_y(yd, -1), step_x(xu, 1), step_x(xd, -1)
    (half_audio,) = call(
        bind(audio_first_kernel), "audio_first", [f32(1024, 768)], totals, rpart, cpart, after, k1, k3,
        h1, l1, h3, l3, pos=pos, scratch=SCALES, flops=1024 * flops,
    )
    yl, yr, xl, xr, half_audio = lax.optimization_barrier((yl, yr, xl, xr, half_audio))
    yu, yd, xu, xd = call(
        bind(near_kernel), "video_near", [f32(264, 768), block, block, block],
        *vectors, k2, ah, al, yl, yr, xl, xr, pos=pos, scratch=SCALES, flops=1024 * flops,
    )
    yu, yd, xu, xd, half_audio = lax.optimization_barrier((yu, yd, xu, xd, half_audio))
    yu, yd, xu, xd = step_y(yu, 1), step_y(yd, -1), step_x(xu, 1), step_x(xd, -1)
    (full_audio,) = call(
        bind(audio_second_kernel), "audio_second", [f32(1024, 768)], *vectors, k2, h2, l2, half_audio,
        pos=pos, scratch=SCALES, flops=1024 * flops,
    )
    unit_audio = lax.psum_scatter(full_audio, "col", scatter_dimension=0, tiled=True)
    after, full_audio = lax.optimization_barrier((tpart, full_audio))
    y_own, x_own = call(
        bind(own_kernel), "video_own", [block, block], totals, rpart, cpart, after, k1, ah, al, pos=pos,
        scratch=SCALES, flops=512 * flops,
    )
    yu, yd, xu, xd, y_own = lax.optimization_barrier((yu, yd, xu, xd, y_own))
    order = pltpu.VMEM((32, 128), F32)
    y1, y2, y3, y0, x1, x2, x3, x0 = call(
        middle_kernel, "video_middle", [f32(72, 768)] * 4 + [f32(64, 768)] * 4,
        tpart, yl, yr, y_own, x_own, yu, yd, xu, xd, pos=pos, scratch=[pltpu.VMEM((256, 768), F32), order],
    )
    y1, y2, y3 = step_x(y1, 1), step_x(y2, 2), step_x(y3, 3)
    x1, x2, x3 = step_y(x1, 1), step_y(x2, 2), step_y(x3, 3)
    (audio_grad,) = call(audio_project_kernel, "audio_grad", [f32(128, 768)], audio, unit_audio)
    video_grad, loss = call(
        bind(video_kernel), "video_grad", [f32(128, 768), f32(1, 1)],
        video, y0, y1, y2, y3, x0, x1, x2, x3, pos=pos, scratch=[order],
    )
    return (loss[0, 0], audio_grad, video_grad)


def solution(mesh):
    in_specs = (P(("row", "col"), None), P(("col", "row"), None))
    out_specs = (P(), P(("row", "col"), None), P(("col", "row"), None))
    return jax.shard_map(local, mesh=mesh, in_specs=in_specs, out_specs=out_specs, check_vma=False)
```

```python
import math

import jax
import jax.numpy as jnp
from jax import lax
from jax.experimental import pallas as pl
from jax.experimental.pallas import tpu as pltpu
from jax.sharding import PartitionSpec as P

ITERS = 3
F32 = jnp.float32
BF16 = jnp.bfloat16
MIB = 1024 * 1024
NEAR = (0, -1, 1, 2)


def vmem():
    return pl.BlockSpec(memory_space=pltpu.VMEM)


def smem():
    return pl.BlockSpec(memory_space=pltpu.SMEM)


def f32(*shape):
    return jax.ShapeDtypeStruct(shape, F32)


def bf16(*shape):
    return jax.ShapeDtypeStruct(shape, BF16)


def call(kernel, name, outs, *args, pos=None, scratch=(), mib=7, flops=0, aliases=None, far_out=False):
    specs = [vmem()] * len(args)
    if pos is not None:
        specs, args = [smem()] + specs, (pos,) + args
    size = lambda arrays: sum(math.prod(a.shape) * a.dtype.itemsize for a in arrays)
    hbm = pl.BlockSpec(memory_space=pltpu.HBM)
    return pl.pallas_call(
        kernel,
        out_shape=[pltpu.HBM(o.shape, o.dtype) if far_out else o for o in outs],
        in_specs=specs,
        out_specs=[hbm if far_out else vmem()] * len(outs),
        scratch_shapes=list(scratch),
        input_output_aliases=aliases or {},
        compiler_params=pltpu.CompilerParams(vmem_limit_bytes=mib * MIB),
        cost_estimate=pl.CostEstimate(
            flops=flops, bytes_accessed=size(args) + size(outs), transcendentals=0
        ),
        name=name,
    )(*args)


def split(value):
    high = value.astype(BF16)
    return high, (value - high.astype(F32)).astype(BF16)


def dot3(lhs, rhs, dims):
    (lh, ll), (rh, rl) = lhs, rhs
    dot = lambda p, q: lax.dot_general(p, q, (dims, ((), ())), preferred_element_type=F32)
    return dot(lh, rh) + (dot(lh, rl) + dot(ll, rh))


def inverse_length(x):
    return lax.rsqrt(jnp.sum(x * x, axis=1, keepdims=True) + 1e-06)


def unit_kernel(a_ref, v_ref, au_ref, vt_ref, vb_ref):
    a = a_ref[...]
    au_ref[...] = a * inverse_length(a)
    v = v_ref[...]
    v = v * inverse_length(v)
    vt_ref[...] = v[:64]
    vb_ref[...] = v[64:]


LAYOUT = (
    ((0, 0), (1, 0)),
    ((0, 1), (0, 2), (1, 1), (1, 2)),
    ((0, 3), (1, 3)),
)


def join_kernel(half, pos_ref, own, left, right, far, out_ref, sems):
    copies = []
    for j, ref in enumerate((own, left, right, far)):
        at = pl.multiple_of(((pos_ref[1 - half] + NEAR[j] + 4) % 4) * 64, 64)
        copies.append(pltpu.make_async_copy(ref, out_ref.at[pl.ds(at, 64), :], sems.at[j]))
        copies[j].start()
    for copy in copies:
        copy.wait()


def halves_kernel(left, right, a_ref, b_ref):
    a_ref[...] = left[0:128, :]
    b_ref[...] = right[128:256, :]


def pieces_body(total, pieces, ah_ref, al_ref, k_ref, vh_ref, vl_ref):
    at = 0
    for piece in pieces:
        rows = slice(at, at + piece.shape[0])
        vh_ref[rows, :], vl_ref[rows, :] = split(piece[...])
        at += piece.shape[0]
        if at % 256 == 0:
            rows = slice(at - 256, at)
            video = (vh_ref[rows, :], vl_ref[rows, :])
            k = jnp.exp(20.0 * dot3(video, (ah_ref[...], al_ref[...]), ((1,), (1,))))
            k_ref[rows, :] = k
            total = total + jnp.sum(k.reshape(-1, 8, k.shape[1]), axis=0)
    return total


def scores_own_kernel(a_ref, p_ref, q_ref, ah_ref, al_ref, k_ref, vh_ref, vl_ref, sum_ref):
    ah_ref[...], al_ref[...] = split(a_ref[...])
    sum_ref[...] = pieces_body(0.0, (p_ref, q_ref), ah_ref, al_ref, k_ref, vh_ref, vl_ref)


def scores_near_kernel(ah_ref, al_ref, in_ref, p0, p1, p2, p3, k_ref, vh_ref, vl_ref, sum_ref):
    sum_ref[...] = pieces_body(in_ref[...], (p0, p1, p2, p3), ah_ref, al_ref, k_ref, vh_ref, vl_ref)


def scores_far_kernel(ah_ref, al_ref, in_ref, p0, p1, q0, q1, k_ref, vh_ref, vl_ref, sum_ref):
    total = pieces_body(in_ref[...], (p0, p1, q0, q1), ah_ref, al_ref, k_ref, vh_ref, vl_ref)
    put_lanes(sum_ref, jnp.sum(total, axis=0, keepdims=True))


def put_lanes(ref, row):
    for m in range(8):
        part = row[:, m * 128 : m * 128 + 128]
        for d in range(8):
            ref[d, m : m + 1, :] = part


def scale_of(part_ref):
    return 1.0 / jnp.sum(part_ref[...], axis=0)


def chunk_of(pos_ref, half, j, b):
    return half * 8 + ((pos_ref[half] + NEAR[j] + 4) % 4) * 2 + b


def chunks(pos_ref, k_refs):
    for ref, blocks in zip(k_refs, LAYOUT):
        for n, (half, j) in enumerate(blocks):
            for b in range(2):
                yield ref, n * 256 + b * 128, chunk_of(pos_ref, half, j, b)


def down(scale_ref, chunk):
    return jnp.broadcast_to(scale_ref[pl.ds(chunk, 1), :], (128, 128)).T


def columns_kernel(pos_ref, part_ref, k1_ref, k2_ref, k3_ref, out_ref):
    r = scale_of(part_ref)
    for ref, at, chunk in chunks(pos_ref, (k1_ref, k2_ref, k3_ref)):
        acc = ref[at : at + 128, 0:128] * r[0:1, :]
        for m in range(1, 8):
            acc = acc + ref[at : at + 128, m * 128 : m * 128 + 128] * r[m : m + 1, :]
        row = jnp.sum(acc.T, axis=0, keepdims=True)
        for d in range(16):
            out_ref[d, pl.ds(chunk, 1), :] = row


def fold(value):
    return jnp.sum(value.reshape(16, 8, 128), axis=0)


def rows_kernel(pos_ref, part_ref, k1_ref, k2_ref, k3_ref, out_ref, scale_ref):
    scale_ref[...] = scale_of(part_ref)
    acc = [0.0] * 8
    for ref, at, chunk in chunks(pos_ref, (k1_ref, k2_ref, k3_ref)):
        c = down(scale_ref, chunk)
        for m in range(8):
            acc[m] = acc[m] + fold(ref[at : at + 128, m * 128 : m * 128 + 128] * c)
    put_lanes(out_ref, jnp.concatenate([jnp.sum(a, axis=0, keepdims=True) for a in acc], axis=1))


def last_rows_kernel(pos_ref, part_ref, rpart_ref, tot_ref, k1_ref, k2_ref, k3_ref, out_ref, scale_ref):
    scale_ref[...] = scale_of(part_ref)
    acc, weighted = [0.0] * 8, [0.0] * 8
    for ref, at, chunk in chunks(pos_ref, (k1_ref, k2_ref, k3_ref)):
        c = down(scale_ref, chunk)
        for m in range(8):
            kernel = ref[at : at + 128, m * 128 : m * 128 + 128]
            prod = kernel * c
            acc[m] = acc[m] + fold(prod)
            weighted[m] = weighted[m] + fold(prod * jnp.log(kernel))
    r = scale_of(rpart_ref)
    logs = jnp.log(jnp.sum(tot_ref[...], axis=0))
    terms = sum(r[m : m + 1] * (weighted[m] - logs[m : m + 1] * acc[m]) for m in range(8))
    put_lanes(out_ref, jnp.concatenate([jnp.sum(a, axis=0, keepdims=True) for a in acc], axis=1))
    for d in range(8):
        out_ref[d, 8:16, :] = terms


def grad_scales(count, tot_ref, rp_ref, cp_ref, tp_ref, c_ref, r_ref, w_ref):
    c_ref[...] = scale_of(cp_ref)
    r = scale_of(rp_ref) * (20.0 / count)
    w = r * jnp.sum(tp_ref[:, 0:8, :], axis=0) / jnp.sum(tot_ref[...], axis=0)
    for m in range(8):
        lanes = slice(m * 128, m * 128 + 128)
        r_ref[:, lanes] = jnp.broadcast_to(r[m : m + 1], (8, 128))
        w_ref[:, lanes] = jnp.broadcast_to(w[m : m + 1], (8, 128))


def grad_block(pos_ref, half, j, k_ref, at, c_ref, r_ref, w_ref):
    c = jnp.concatenate([down(c_ref, chunk_of(pos_ref, half, j, b)) for b in range(2)], axis=0)
    c = jnp.concatenate([c] * 8, axis=1)
    return split(k_ref[at : at + 256, :] * (w_ref[0:1, :] - r_ref[0:1, :] * c))


SCALES = [pltpu.VMEM((16, 128), F32), pltpu.VMEM((8, 1024), F32), pltpu.VMEM((8, 1024), F32)]


def far_kernel(count, pos_ref, tot_ref, rp_ref, cp_ref, tp_ref, k_ref, ah_ref, al_ref,
               yu_ref, yd_ref, xu_ref, xd_ref, c_ref, r_ref, w_ref):
    grad_scales(count, tot_ref, rp_ref, cp_ref, tp_ref, c_ref, r_ref, w_ref)
    for half, (u_ref, d_ref) in enumerate(((yu_ref, yd_ref), (xu_ref, xd_ref))):
        g = grad_block(pos_ref, half, 3, k_ref, half * 256, c_ref, r_ref, w_ref)
        out = dot3(g, (ah_ref[...], al_ref[...]), ((1,), (0,)))
        u_ref[0:128, :] = out[:128]
        d_ref[0:128, :] = out[128:]
    terms = jnp.concatenate([jnp.sum(tp_ref[:, 8:16, :], axis=0)] * 6, axis=1)
    yu_ref[128:136, :] = terms
    yd_ref[128:136, :] = terms


def audio_body(pos_ref, layouts, start, u_ref, c_ref, r_ref, w_ref, copies=None):
    for k_ref, h_ref, l_ref, first, blocks in layouts:
        for n, (half, j) in enumerate(blocks, first):
            at = slice(n * 256, n * 256 + 256)
            g = grad_block(pos_ref, half, j, k_ref, n * 256, c_ref, r_ref, w_ref)
            for m in range(4):
                lanes = slice(m * 256, m * 256 + 256)
                part = tuple(v[:, lanes] for v in g)
                out = dot3(part, (h_ref[at, :], l_ref[at, :]), ((0,), (0,)))
                u_ref[lanes, :] = out if start is None else start[lanes, :] + out
                if copies is not None and n == first + len(blocks) - 1:
                    copies[m].start()
            start = u_ref


def audio_first_kernel(count, pos_ref, tot_ref, rp_ref, cp_ref, tp_ref, k1_ref, k2_ref, k3_ref,
                       h1_ref, l1_ref, h2_ref, l2_ref, h3_ref, l3_ref, u_ref, c_ref, r_ref, w_ref):
    grad_scales(count, tot_ref, rp_ref, cp_ref, tp_ref, c_ref, r_ref, w_ref)
    layouts = (
        (k1_ref, h1_ref, l1_ref, 0, LAYOUT[0]),
        (k3_ref, h3_ref, l3_ref, 0, LAYOUT[2]),
        (k2_ref, h2_ref, l2_ref, 0, LAYOUT[1][:2]),
    )
    audio_body(pos_ref, layouts, None, u_ref, c_ref, r_ref, w_ref)


def audio_second_kernel(count, pos_ref, tot_ref, rp_ref, cp_ref, tp_ref, k2_ref, h2_ref, l2_ref,
                        in_ref, u_ref, c_ref, r_ref, w_ref, sum_ref, sems):
    grad_scales(count, tot_ref, rp_ref, cp_ref, tp_ref, c_ref, r_ref, w_ref)
    copies = [
        pltpu.make_async_copy(
            sum_ref.at[pl.ds(m * 256, 256), :], u_ref.at[pl.ds(m * 256, 256), :], sems.at[m]
        )
        for m in range(4)
    ]
    layouts = ((k2_ref, h2_ref, l2_ref, 2, LAYOUT[1][2:]),)
    audio_body(pos_ref, layouts, in_ref, sum_ref, c_ref, r_ref, w_ref, copies)
    for copy in copies:
        copy.wait()


def near_kernel(count, pos_ref, tot_ref, rp_ref, cp_ref, tp_ref, k_ref, ah_ref, al_ref,
                yl_ref, yr_ref, xl_ref, xr_ref, yu_out, yd_out, xu_out, xd_out, c_ref, r_ref, w_ref,
                yu_ref, yd_ref, xu_ref, xd_ref, sems):
    grad_scales(count, tot_ref, rp_ref, cp_ref, tp_ref, c_ref, r_ref, w_ref)
    yu_ref[256:264, :] = yl_ref[128:136, :]
    copies = []
    for n, (ref, left, right, target) in enumerate((
        (yd_ref, None, yr_ref, yd_out), (yu_ref, yl_ref, None, yu_out),
        (xd_ref, None, xr_ref, xd_out), (xu_ref, xl_ref, None, xu_out),
    )):
        half, j = LAYOUT[1][n]
        g = grad_block(pos_ref, half, j, k_ref, n * 256, c_ref, r_ref, w_ref)
        out = dot3(g, (ah_ref[...], al_ref[...]), ((1,), (0,)))
        ref[0:128, :] = out[:128] if left is None else out[:128] + left[0:128, :]
        ref[128:256, :] = out[128:] if right is None else out[128:] + right[0:128, :]
        copies.append(pltpu.make_async_copy(ref, target, sems.at[n]))
        copies[n].start()
    for copy in copies:
        copy.wait()


def own_kernel(count, pos_ref, tot_ref, rp_ref, cp_ref, tp_ref, k_ref, ah_ref, al_ref,
               y_ref, x_ref, c_ref, r_ref, w_ref):
    grad_scales(count, tot_ref, rp_ref, cp_ref, tp_ref, c_ref, r_ref, w_ref)
    for half, ref in enumerate((y_ref, x_ref)):
        g = grad_block(pos_ref, half, 0, k_ref, half * 256, c_ref, r_ref, w_ref)
        ref[...] = dot3(g, (ah_ref[...], al_ref[...]), ((1,), (0,)))


def ordered_sum(me, values, order_ref):
    for k, value in enumerate(values):
        order_ref[pl.ds(pl.multiple_of(((me + k) % 4) * 8, 8), 8), :] = value
    return jnp.sum(order_ref[...].reshape(4, 8, 128), axis=0)


def middle_kernel(pos_ref, tp_ref, yl_ref, yr_ref, y_ref, x_ref, yu_ref, yd_ref, xu_ref, xd_ref,
                  y1_ref, y2_ref, y3_ref, y0_ref, x1_ref, x2_ref, x3_ref, x0_ref, sum_ref, order_ref):
    terms = ordered_sum(
        pos_ref[0],
        (jnp.sum(tp_ref[:, 8:16, :], axis=0), yr_ref[128:136, 0:128], yu_ref[256:264, 0:128],
         yl_ref[128:136, 0:128]),
        order_ref,
    )
    for half, (own, up, down, outs) in enumerate((
        (y_ref, yu_ref, yd_ref, (y0_ref, y1_ref, y2_ref, y3_ref)),
        (x_ref, xu_ref, xd_ref, (x0_ref, x1_ref, x2_ref, x3_ref)),
    )):
        sum_ref[...] = own[...] + up[0:256, :] + down[...]
        for k, ref in enumerate(outs):
            at = ((pos_ref[1 - half] + k) % 4) * 64
            ref[0:64, :] = sum_ref[pl.ds(pl.multiple_of(at, 64), 64), :]
            if half == 0:
                ref[64:72, :] = jnp.concatenate([terms] * 6, axis=1)


def project(x, grad):
    inv = inverse_length(x)
    unit = x * inv
    return (grad - unit * jnp.sum(unit * grad, axis=1, keepdims=True)) * inv


def video_kernel(count, pos_ref, v_ref, y0, y1, y2, y3, x0, x1, x2, x3, out_ref, loss_ref, order_ref):
    top = y0[0:64, :] + y1[0:64, :] + y2[0:64, :] + y3[0:64, :]
    bottom = x0[...] + x1[...] + x2[...] + x3[...]
    out_ref[0:64, :] = project(v_ref[0:64, :], top)
    out_ref[64:128, :] = project(v_ref[64:128, :], bottom)
    terms = ordered_sum(
        pos_ref[1], tuple(ref[64:72, 0:128] for ref in (y0, y3, y2, y1)), order_ref
    )
    loss_ref[...] = jnp.full((1, 1), -jnp.sum(terms) / count)


def audio_project_kernel(x_ref, grad_ref, out_ref):
    out_ref[...] = project(x_ref[...], grad_ref[...])


def step_y(v, k):
    return lax.ppermute(v, "row", [(i, ((i // 4 + k) % 4) * 4 + i % 4) for i in range(16)])


def step_x(v, k):
    return lax.ppermute(v, "row", [(i, (i // 4) * 4 + (i % 4 + k) % 4) for i in range(16)])


def swap(part, axis):
    return lax.all_to_all(part, axis, 0, 0, tiled=True)


def local(audio, video):
    count = audio.shape[0] * 128
    bind = lambda kernel: lambda *refs: kernel(count, *refs)
    row = lax.axis_index("row")
    pos = jnp.stack([row // 4, row % 4]).astype(jnp.int32)
    audio_unit, vt, vb = call(
        unit_kernel, "unit_rows", [f32(128, 768), f32(64, 768), f32(64, 768)],
        *(pltpu.with_memory_space_constraint(a, pltpu.HBM) for a in (audio, video)),
    )
    audio_tile = lax.all_gather(audio_unit, "col", axis=0, tiled=True)
    join = lambda half, *parts: call(
        lambda *refs: join_kernel(half, *refs), "join", [f32(256, 768)], *parts, pos=pos, mib=4,
        far_out=True, scratch=[pltpu.SemaphoreType.DMA((4,))],
    )[0]
    xl, xr, yl, yr = step_x(vt, 1), step_x(vt, -1), step_y(vb, 1), step_y(vb, -1)
    yr, xl, xr = lax.optimization_barrier((yr, xl, xr))
    first = join(0, vt, xl, xr, step_x(xl, 1))
    second = join(1, vb, yl, yr, step_y(yr, -1))
    fl, fr, sl, sr = step_y(first, 1), step_y(first, -1), step_x(second, 1), step_x(second, -1)
    flops = 3 * 2 * 1024 * 768
    ah, al, k1, h1, l1, sums = call(
        scores_own_kernel, "scores_own",
        [bf16(1024, 768), bf16(1024, 768), f32(512, 1024), bf16(512, 768), bf16(512, 768), f32(8, 1024)],
        audio_tile, first, second, flops=512 * flops,
    )
    halves = lambda left, right: call(halves_kernel, "halves", [f32(128, 768)] * 2, left, right, mib=4)
    sl, sr, sums = lax.optimization_barrier((sl, sr, sums))
    c, d = halves(sl, sr)
    fl, fr, c = lax.optimization_barrier((fl, fr, c))
    a, b = halves(fl, fr)
    far = (step_y(a, 1), step_y(b, -1), step_x(c, 1), step_x(d, -1))
    k2, h2, l2, sums = call(
        scores_near_kernel, "scores_near",
        [f32(1024, 1024), bf16(1024, 768), bf16(1024, 768), f32(8, 1024)],
        ah, al, sums, fl, fr, sl, sr, flops=1024 * flops,
    )
    k3, h3, l3, part = call(
        scores_far_kernel, "scores_far",
        [f32(512, 1024), bf16(512, 768), bf16(512, 768), f32(8, 8, 128)],
        ah, al, sums, *far, flops=512 * flops,
    )
    ks = (k1, k2, k3)
    scale = pltpu.VMEM((16, 128), F32)
    totals = swap(part, "col")
    rpart = totals
    for step in range(ITERS):
        cpart = swap(call(columns_kernel, "column_sums", [f32(16, 16, 128)], rpart, *ks, pos=pos, mib=9)[0], "row")
        if step < ITERS - 1:
            part = call(rows_kernel, "row_sums", [f32(8, 8, 128)], cpart, *ks, pos=pos, mib=9, scratch=[scale])[0]
            rpart = swap(part, "col")
    part = call(last_rows_kernel, "row_sums_and_loss", [f32(8, 16, 128)], cpart, rpart, totals, *ks,
                pos=pos, mib=9, scratch=[scale])[0]
    tpart = swap(part, "col")

    vectors = (totals, rpart, cpart, tpart)
    block = f32(256, 768)
    yu, yd, xu, xd = call(
        bind(far_kernel), "video_far", [f32(136, 768), f32(136, 768), f32(128, 768), f32(128, 768)],
        *vectors, k3, ah, al, pos=pos, scratch=SCALES, flops=512 * flops,
    )
    after, yu = lax.optimization_barrier((tpart, yu))
    yl, yr, xl, xr = step_y(yu, 1), step_y(yd, -1), step_x(xu, 1), step_x(xd, -1)
    (half_audio,) = call(
        bind(audio_first_kernel), "audio_first", [f32(1024, 768)], totals, rpart, cpart, after, *ks,
        h1, l1, h2, l2, h3, l3, pos=pos, scratch=SCALES, flops=1024 * flops,
    )
    yl, yr, xl, xr, half_audio = lax.optimization_barrier((yl, yr, xl, xr, half_audio))
    yu, yd, xu, xd = call(
        bind(near_kernel), "video_near", [f32(264, 768), block, block, block],
        *vectors, k2, ah, al, yl, yr, xl, xr, pos=pos, flops=1024 * flops, mib=12, far_out=True,
        scratch=SCALES + [pltpu.VMEM((264, 768), F32)] + [pltpu.VMEM((256, 768), F32)] * 3
        + [pltpu.SemaphoreType.DMA((4,))],
    )
    yu, yd, xu, xd, half_audio = lax.optimization_barrier((yu, yd, xu, xd, half_audio))
    yu, yd, xu, xd = step_y(yu, 1), step_y(yd, -1), step_x(xu, 1), step_x(xd, -1)
    (full_audio,) = call(
        bind(audio_second_kernel), "audio_second", [f32(1024, 768)], *vectors, k2, h2, l2, half_audio,
        pos=pos, scratch=SCALES + [pltpu.VMEM((1024, 768), F32), pltpu.SemaphoreType.DMA((4,))],
        flops=1024 * flops, mib=12, far_out=True,
    )
    unit_audio = lax.psum_scatter(full_audio, "col", scatter_dimension=0, tiled=True)
    after, full_audio = lax.optimization_barrier((tpart, full_audio))
    y_own, x_own = call(
        bind(own_kernel), "video_own", [block, block], totals, rpart, cpart, after, k1, ah, al, pos=pos,
        scratch=SCALES, flops=512 * flops,
    )
    yu, yd, xu, xd, y_own = lax.optimization_barrier((yu, yd, xu, xd, y_own))
    order = pltpu.VMEM((32, 128), F32)
    y1, y2, y3, y0, x1, x2, x3, x0 = call(
        middle_kernel, "video_middle", [f32(72, 768)] * 4 + [f32(64, 768)] * 4,
        tpart, yl, yr, y_own, x_own, yu, yd, xu, xd, pos=pos, scratch=[pltpu.VMEM((256, 768), F32), order],
    )
    y1, y2, y3 = step_x(y1, 1), step_x(y2, 2), step_x(y3, 3)
    x1, x2, x3 = step_y(x1, 1), step_y(x2, 2), step_y(x3, 3)
    unit_audio, x1 = lax.optimization_barrier((unit_audio, x1))
    (audio_grad,) = call(audio_project_kernel, "audio_grad", [f32(128, 768)], audio, unit_audio)
    video_grad, loss = call(
        bind(video_kernel), "video_grad", [f32(128, 768), f32(1, 1)],
        video, y0, y1, y2, y3, x0, x1, x2, x3, pos=pos, scratch=[order],
    )
    return (loss[0, 0], audio_grad, video_grad)


def solution(mesh):
    in_specs = (P(("row", "col"), None), P(("col", "row"), None))
    out_specs = (P(), P(("row", "col"), None), P(("col", "row"), None))
    return jax.shard_map(local, mesh=mesh, in_specs=in_specs, out_specs=out_specs, check_vma=False)
```

```python
import jax
import jax.numpy as jnp
from jax import lax
from jax.experimental import pallas as pl
from jax.experimental.pallas import tpu as pltpu
from jax.sharding import PartitionSpec as P

ITERS = 3
F32 = jnp.float32
BF16 = jnp.bfloat16
MIB = 1024 * 1024
NEAR = (0, -1, 1, 2)


def vmem():
    return pl.BlockSpec(memory_space=pltpu.VMEM)


def smem():
    return pl.BlockSpec(memory_space=pltpu.SMEM)


def f32(*shape):
    return jax.ShapeDtypeStruct(shape, F32)


def bf16(*shape):
    return jax.ShapeDtypeStruct(shape, BF16)


def call(kernel, name, outs, *args, pos=None, scratch=(), mib=20, flops=0, light=False):
    specs = [vmem()] * len(args)
    if pos is not None:
        specs, args = [smem()] + specs, (pos,) + args
    size = lambda arrays: sum(a.size * a.dtype.itemsize for a in arrays)
    cost = pl.CostEstimate(
        flops=0 if light else flops,
        bytes_accessed=0 if light else size(args) + size(outs),
        transcendentals=0,
    )
    return pl.pallas_call(
        kernel,
        out_shape=list(outs),
        in_specs=specs,
        out_specs=[vmem()] * len(outs),
        scratch_shapes=list(scratch),
        compiler_params=pltpu.CompilerParams(vmem_limit_bytes=mib * MIB),
        cost_estimate=cost,
        name=name,
    )(*args)


def split(value):
    high = value.astype(BF16)
    return high, (value - high.astype(F32)).astype(BF16)


def dot3(lhs, rhs, dims):
    (lh, ll), (rh, rl) = lhs, rhs
    dot = lambda p, q: lax.dot_general(p, q, (dims, ((), ())), preferred_element_type=F32)
    return dot(lh, rh) + (dot(lh, rl) + dot(ll, rh))


def inverse_length(x):
    return lax.rsqrt(jnp.sum(x * x, axis=1, keepdims=True) + 1e-06)


def unit_kernel(a_ref, v_ref, au_ref, vt_ref, vb_ref):
    a = a_ref[...]
    au_ref[...] = a * inverse_length(a)
    v = v_ref[...]
    v = v * inverse_length(v)
    vt_ref[...] = v[:64]
    vb_ref[...] = v[64:]


LAYOUT = (
    ((0, 0), (1, 0)),
    ((0, 1), (0, 2), (1, 1), (1, 2)),
    ((0, 3), (1, 3)),
)


def join_kernel(axis, pos_ref, own, left, right, far, out_ref):
    size = own.shape[0]
    for j, ref in enumerate((own, left, right, far)):
        at = ((pos_ref[axis] + NEAR[j] + 4) % 4) * size
        out_ref[pl.ds(pl.multiple_of(at, size), size), :] = ref[...]


def halves_kernel(left, right, a_ref, b_ref):
    a_ref[...] = left[0:128, :]
    b_ref[...] = right[128:256, :]


def pieces_body(total, pieces, ah_ref, al_ref, k_ref, vh_ref, vl_ref):
    at = 0
    for piece in pieces:
        rows = slice(at, at + piece.shape[0])
        vh_ref[rows, :], vl_ref[rows, :] = split(piece[...])
        at += piece.shape[0]
        if at % 256 == 0:
            rows = slice(at - 256, at)
            video = (vh_ref[rows, :], vl_ref[rows, :])
            k = jnp.exp(20.0 * dot3(video, (ah_ref[...], al_ref[...]), ((1,), (1,))))
            k_ref[rows, :] = k
            total = total + jnp.sum(k.reshape(-1, 8, k.shape[1]), axis=0)
    return total


def scores_own_kernel(a_ref, b_ref, p_ref, q_ref, ah_ref, al_ref, k_ref, vh_ref, vl_ref, sum_ref):
    ah_ref[0:512, :], al_ref[0:512, :] = split(a_ref[...])
    ah_ref[512:1024, :], al_ref[512:1024, :] = split(b_ref[...])
    sum_ref[...] = pieces_body(0.0, (p_ref, q_ref), ah_ref, al_ref, k_ref, vh_ref, vl_ref)


def scores_near_kernel(ah_ref, al_ref, in_ref, p0, p1, p2, p3, k_ref, vh_ref, vl_ref, sum_ref):
    sum_ref[...] = pieces_body(in_ref[...], (p0, p1, p2, p3), ah_ref, al_ref, k_ref, vh_ref, vl_ref)


def scores_far_kernel(pos_ref, ah_ref, al_ref, in_ref, p0, p1, q0, q1, k_ref, vh_ref, vl_ref, sum_ref):
    total = pieces_body(in_ref[...], (p0, p1, q0, q1), ah_ref, al_ref, k_ref, vh_ref, vl_ref)
    put_lanes(pos_ref, sum_ref, jnp.sum(total, axis=0, keepdims=True))


def put_lanes(pos_ref, ref, row):
    for d in range(8):
        swapped = 4 * ((pos_ref[3] + d) % 2)
        for m in range(8):
            ref[d, pl.ds((m + swapped) % 8, 1), :] = row[:, m * 128 : m * 128 + 128]


def scale_of(part_ref):
    return 1.0 / jnp.sum(part_ref[...], axis=0)


def chunk_of(pos_ref, half, j, b):
    return half * 8 + ((pos_ref[half] + NEAR[j] + 4) % 4) * 2 + b


def chunks(pos_ref, k_refs):
    for ref, blocks in zip(k_refs, LAYOUT):
        for n, (half, j) in enumerate(blocks):
            for b in range(2):
                yield ref, n * 256 + b * 128, chunk_of(pos_ref, half, j, b)


def down(scale_ref, chunk):
    return jnp.broadcast_to(scale_ref[pl.ds(chunk, 1), :], (128, 128)).T


def columns_kernel(pos_ref, part_ref, k1_ref, k2_ref, k3_ref, out_ref):
    r = scale_of(part_ref)
    for ref, at, chunk in chunks(pos_ref, (k1_ref, k2_ref, k3_ref)):
        acc = ref[at : at + 128, 0:128] * r[0:1, :]
        for m in range(1, 8):
            acc = acc + ref[at : at + 128, m * 128 : m * 128 + 128] * r[m : m + 1, :]
        row = jnp.sum(acc.T, axis=0, keepdims=True)
        for d in range(16):
            out_ref[d, pl.ds(chunk, 1), :] = row


def fold(value):
    return jnp.sum(value.reshape(16, 8, 128), axis=0)


def rows_kernel(pos_ref, part_ref, k1_ref, k2_ref, k3_ref, out_ref, scale_ref):
    scale_ref[...] = scale_of(part_ref)
    acc = [0.0] * 8
    for ref, at, chunk in chunks(pos_ref, (k1_ref, k2_ref, k3_ref)):
        c = down(scale_ref, chunk)
        for m in range(8):
            acc[m] = acc[m] + fold(ref[at : at + 128, m * 128 : m * 128 + 128] * c)
    put_lanes(pos_ref, out_ref, jnp.concatenate([jnp.sum(a, axis=0, keepdims=True) for a in acc], axis=1))


def last_rows_kernel(pos_ref, part_ref, rpart_ref, tot_ref, k1_ref, k2_ref, k3_ref, out_ref, scale_ref):
    scale_ref[...] = scale_of(part_ref)
    acc, weighted = [0.0] * 8, [0.0] * 8
    for ref, at, chunk in chunks(pos_ref, (k1_ref, k2_ref, k3_ref)):
        c = down(scale_ref, chunk)
        for m in range(8):
            kernel = ref[at : at + 128, m * 128 : m * 128 + 128]
            prod = kernel * c
            acc[m] = acc[m] + fold(prod)
            weighted[m] = weighted[m] + fold(prod * jnp.log(kernel))
    r = scale_of(rpart_ref)
    logs = jnp.log(jnp.sum(tot_ref[...], axis=0))
    terms = sum(r[m : m + 1] * (weighted[m] - logs[m : m + 1] * acc[m]) for m in range(8))
    put_lanes(pos_ref, out_ref, jnp.concatenate([jnp.sum(a, axis=0, keepdims=True) for a in acc], axis=1))
    for d in range(8):
        out_ref[d, 8:16, :] = terms


def grad_scales(count, tot_ref, rp_ref, cp_ref, tp_ref, c_ref, r_ref, w_ref):
    c_ref[...] = scale_of(cp_ref)
    r = scale_of(rp_ref) * (20.0 / count)
    w = r * jnp.sum(tp_ref[:, 0:8, :], axis=0) / jnp.sum(tot_ref[...], axis=0)
    for m in range(8):
        lanes = slice(m * 128, m * 128 + 128)
        r_ref[:, lanes] = jnp.broadcast_to(r[m : m + 1], (8, 128))
        w_ref[:, lanes] = jnp.broadcast_to(w[m : m + 1], (8, 128))


def grad_block(pos_ref, half, j, k_ref, at, c_ref, r_ref, w_ref):
    c = jnp.concatenate([down(c_ref, chunk_of(pos_ref, half, j, b)) for b in range(2)], axis=0)
    c = jnp.concatenate([c] * 8, axis=1)
    return split(k_ref[at : at + 256, :] * (w_ref[0:1, :] - r_ref[0:1, :] * c))


SCALES = [pltpu.VMEM((16, 128), F32), pltpu.VMEM((8, 1024), F32), pltpu.VMEM((8, 1024), F32)]


def far_kernel(count, pos_ref, tot_ref, rp_ref, cp_ref, tp_ref, k_ref, ah_ref, al_ref,
               yu_ref, yd_ref, xu_ref, xd_ref, c_ref, r_ref, w_ref):
    grad_scales(count, tot_ref, rp_ref, cp_ref, tp_ref, c_ref, r_ref, w_ref)
    for half, (u_ref, d_ref) in enumerate(((yu_ref, yd_ref), (xu_ref, xd_ref))):
        g = grad_block(pos_ref, half, 3, k_ref, half * 256, c_ref, r_ref, w_ref)
        out = dot3(g, (ah_ref[...], al_ref[...]), ((1,), (0,)))
        u_ref[0:128, :] = out[:128]
        d_ref[0:128, :] = out[128:]
    terms = jnp.concatenate([jnp.sum(tp_ref[:, 8:16, :], axis=0)] * 6, axis=1)
    yu_ref[128:136, :] = terms
    yd_ref[128:136, :] = terms


def audio_body(pos_ref, layouts, start, u_ref, c_ref, r_ref, w_ref, outs):
    for k_ref, h_ref, l_ref, first, blocks in layouts:
        for n, (half, j) in enumerate(blocks, first):
            at = slice(n * 256, n * 256 + 256)
            g = grad_block(pos_ref, half, j, k_ref, n * 256, c_ref, r_ref, w_ref)
            for m in range(4):
                lanes = slice(m * 256, m * 256 + 256)
                part = tuple(v[:, lanes] for v in g)
                out = dot3(part, (h_ref[at, :], l_ref[at, :]), ((0,), (0,)))
                out = out if start is None else start[lanes, :] + out
                if k_ref is layouts[-1][0] and n == first + len(blocks) - 1:
                    outs[m // 2][m % 2 * 256 : m % 2 * 256 + 256, :] = out
                else:
                    u_ref[lanes, :] = out
            start = u_ref


def audio_kernel(count, pos_ref, tot_ref, rp_ref, cp_ref, tp_ref, k1_ref, k2_ref, k3_ref,
                 h1_ref, l1_ref, h2_ref, l2_ref, h3_ref, l3_ref, mine_ref, other_ref,
                 c_ref, r_ref, w_ref, u_ref):
    grad_scales(count, tot_ref, rp_ref, cp_ref, tp_ref, c_ref, r_ref, w_ref)
    layouts = (
        (k1_ref, h1_ref, l1_ref, 0, LAYOUT[0]),
        (k3_ref, h3_ref, l3_ref, 0, LAYOUT[2]),
        (k2_ref, h2_ref, l2_ref, 0, LAYOUT[1]),
    )
    audio_body(pos_ref, layouts, None, u_ref, c_ref, r_ref, w_ref, (mine_ref, other_ref))


def near_kernel(count, pos_ref, tot_ref, rp_ref, cp_ref, tp_ref, k_ref, ah_ref, al_ref,
                yl_ref, yr_ref, xl_ref, xr_ref, yu_ref, yd_ref, xu_ref, xd_ref, c_ref, r_ref, w_ref):
    grad_scales(count, tot_ref, rp_ref, cp_ref, tp_ref, c_ref, r_ref, w_ref)
    for n, (ref, left, right) in enumerate((
        (yd_ref, None, yr_ref), (yu_ref, yl_ref, None), (xd_ref, None, xr_ref), (xu_ref, xl_ref, None)
    )):
        half, j = LAYOUT[1][n]
        g = grad_block(pos_ref, half, j, k_ref, n * 256, c_ref, r_ref, w_ref)
        out = dot3(g, (ah_ref[...], al_ref[...]), ((1,), (0,)))
        ref[0:128, :] = out[:128] if left is None else out[:128] + left[0:128, :]
        ref[128:256, :] = out[128:] if right is None else out[128:] + right[0:128, :]
    yu_ref[256:264, :] = yl_ref[128:136, :]


def own_kernel(count, pos_ref, tot_ref, rp_ref, cp_ref, tp_ref, k_ref, ah_ref, al_ref,
               y_ref, x_ref, c_ref, r_ref, w_ref):
    grad_scales(count, tot_ref, rp_ref, cp_ref, tp_ref, c_ref, r_ref, w_ref)
    for half, ref in enumerate((y_ref, x_ref)):
        g = grad_block(pos_ref, half, 0, k_ref, half * 256, c_ref, r_ref, w_ref)
        ref[...] = dot3(g, (ah_ref[...], al_ref[...]), ((1,), (0,)))


def ordered_sum(me, values, order_ref):
    for k, value in enumerate(values):
        order_ref[pl.ds(pl.multiple_of(((me + k) % 4) * 8, 8), 8), :] = value
    return jnp.sum(order_ref[...].reshape(4, 8, 128), axis=0)


def middle_kernel(pos_ref, tp_ref, yl_ref, yr_ref, y_ref, x_ref, yu_ref, yd_ref, xu_ref, xd_ref,
                  y1_ref, y2_ref, y3_ref, y0_ref, x1_ref, x2_ref, x3_ref, x0_ref, sum_ref, order_ref):
    terms = ordered_sum(
        pos_ref[0],
        (jnp.sum(tp_ref[:, 8:16, :], axis=0), yr_ref[128:136, 0:128], yu_ref[256:264, 0:128],
         yl_ref[128:136, 0:128]),
        order_ref,
    )
    for half, (own, up, down, outs) in enumerate((
        (y_ref, yu_ref, yd_ref, (y0_ref, y1_ref, y2_ref, y3_ref)),
        (x_ref, xu_ref, xd_ref, (x0_ref, x1_ref, x2_ref, x3_ref)),
    )):
        sum_ref[...] = own[...] + up[0:256, :] + down[...]
        for k, ref in enumerate(outs):
            at = ((pos_ref[1 - half] + k) % 4) * 64
            ref[0:64, :] = sum_ref[pl.ds(pl.multiple_of(at, 64), 64), :]
            if half == 0:
                ref[64:72, :] = jnp.concatenate([terms] * 6, axis=1)


def audio_sum_kernel(pos_ref, mine_ref, got_ref, far_ref, up_ref, down_ref, own_ref):
    for k, ref in ((2, far_ref), (1, up_ref), (3, down_ref), (0, own_ref)):
        at = pl.ds(pl.multiple_of(((pos_ref[2] + k) % 4) * 128, 128), 128)
        ref[...] = mine_ref[at, :] + got_ref[at, :]


def add_kernel(a_ref, b_ref, out_ref):
    out_ref[...] = a_ref[...] + b_ref[...]


def project(x, grad):
    inv = inverse_length(x)
    unit = x * inv
    return (grad - unit * jnp.sum(unit * grad, axis=1, keepdims=True)) * inv


def video_kernel(count, pos_ref, v_ref, y0, y1, y2, y3, x0, x1, x2, x3, out_ref, loss_ref, order_ref):
    top = y0[0:64, :] + y1[0:64, :] + y2[0:64, :] + y3[0:64, :]
    bottom = x0[...] + x1[...] + x2[...] + x3[...]
    out_ref[0:64, :] = project(v_ref[0:64, :], top)
    out_ref[64:128, :] = project(v_ref[64:128, :], bottom)
    terms = ordered_sum(
        pos_ref[1], tuple(ref[64:72, 0:128] for ref in (y0, y3, y2, y1)), order_ref
    )
    loss_ref[...] = jnp.full((1, 1), -jnp.sum(terms) / count)


def audio_project_kernel(x_ref, own_ref, up_ref, down_ref, out_ref):
    out_ref[...] = project(x_ref[...], own_ref[...] + up_ref[...] + down_ref[...])


def step_y(v, k):
    return lax.ppermute(v, "row", [(i, ((i // 4 + k) % 4) * 4 + i % 4) for i in range(16)])


def step_x(v, k):
    return lax.ppermute(v, "row", [(i, (i // 4) * 4 + (i % 4 + k) % 4) for i in range(16)])


def step_z(v, k):
    return lax.ppermute(v, "col", [(i, ((i // 2 + k) % 4) * 2 + i % 2) for i in range(8)])


def other_core(v):
    return lax.ppermute(v, "col", [(i, i ^ 1) for i in range(8)])


def swap(part, axis):
    return lax.all_to_all(part, axis, 0, 0, tiled=True)


def local(audio, video):
    count = audio.shape[0] * 128
    bind = lambda kernel: lambda *refs: kernel(count, *refs)
    row = lax.axis_index("row")
    col = lax.axis_index("col")
    pos = jnp.stack([row // 4, row % 4, col // 2, col % 2]).astype(jnp.int32)
    audio_unit, vt, vb = call(
        unit_kernel, "unit_rows", [f32(128, 768), f32(64, 768), f32(64, 768)],
        *(pltpu.with_memory_space_constraint(a, pltpu.HBM) for a in (audio, video)),
    )
    join = lambda axis, *parts: call(
        lambda *refs: join_kernel(axis, *refs), "join", [f32(4 * parts[0].shape[0], 768)], *parts, pos=pos, mib=8
    )[0]
    xl, xr, yl, yr = step_x(vt, 1), step_x(vt, -1), step_y(vb, 1), step_y(vb, -1)
    zl, zr = step_z(audio_unit, 1), step_z(audio_unit, -1)
    yr, xl, xr = lax.optimization_barrier((yr, xl, xr))
    first = join(1, vt, xl, xr, step_x(xl, 1))
    second = join(0, vb, yl, yr, step_y(yr, -1))
    zl, _, _ = lax.optimization_barrier((zl, first, second))
    fl, fr, sl, sr = step_y(first, 1), step_y(first, -1), step_x(second, 1), step_x(second, -1)
    zf = lax.optimization_barrier((step_z(zl, 1), fl, fr, sl, sr))[0]
    audio_own = join(2, audio_unit, zl, zr, zf)
    audio_other = other_core(audio_own)
    flops = 3 * 2 * 1024 * 768
    ah, al, k1, h1, l1, sums = call(
        scores_own_kernel, "scores_own",
        [bf16(1024, 768), bf16(1024, 768), f32(512, 1024), bf16(512, 768), bf16(512, 768), f32(8, 1024)],
        audio_own, audio_other, first, second, light=True,
    )
    halves = lambda left, right: call(halves_kernel, "halves", [f32(128, 768)] * 2, left, right, mib=8)
    c, d = halves(sl, sr)
    fl, fr, c = lax.optimization_barrier((fl, fr, c))
    a, b = halves(fl, fr)
    far = (step_y(a, 1), step_y(b, -1), step_x(c, 1), step_x(d, -1))
    k2, h2, l2, sums = call(
        scores_near_kernel, "scores_near",
        [f32(1024, 1024), bf16(1024, 768), bf16(1024, 768), f32(8, 1024)],
        ah, al, sums, fl, fr, sl, sr, light=True,
    )
    k3, h3, l3, part = call(
        scores_far_kernel, "scores_far",
        [f32(512, 1024), bf16(512, 768), bf16(512, 768), f32(8, 8, 128)],
        ah, al, sums, *far, pos=pos, light=True,
    )
    ks = (k1, k2, k3)
    scale = pltpu.VMEM((16, 128), F32)
    totals = swap(part, "col")
    rpart = totals
    for step in range(ITERS):
        cpart = swap(call(columns_kernel, "column_sums", [f32(16, 16, 128)], rpart, *ks, pos=pos, mib=14)[0], "row")
        if step < ITERS - 1:
            part = call(rows_kernel, "row_sums", [f32(8, 8, 128)], cpart, *ks, pos=pos, mib=14, scratch=[scale])[0]
            rpart = swap(part, "col")
    part = call(last_rows_kernel, "row_sums_and_loss", [f32(8, 16, 128)], cpart, rpart, totals, *ks,
                pos=pos, mib=14, scratch=[scale])[0]
    tpart = swap(part, "col")

    vectors = (totals, rpart, cpart, tpart)
    block = f32(256, 768)
    yu, yd, xu, xd = call(
        bind(far_kernel), "video_far", [f32(136, 768), f32(136, 768), f32(128, 768), f32(128, 768)],
        *vectors, k3, ah, al, pos=pos, scratch=SCALES, flops=512 * flops,
    )
    after, yu = lax.optimization_barrier((tpart, yu))
    yl, yr, xl, xr = step_y(yu, 1), step_y(yd, -1), step_x(xu, 1), step_x(xd, -1)
    mine, other = call(
        bind(audio_kernel), "audio_all", [f32(512, 768)] * 2, totals, rpart, cpart, after, *ks,
        h1, l1, h2, l2, h3, l3, pos=pos, scratch=SCALES + [pltpu.VMEM((1024, 768), F32)],
        flops=2048 * flops, mib=28,
    )
    yl, yr, xl, xr, mine, other = lax.optimization_barrier((yl, yr, xl, xr, mine, other))
    got = other_core(other)
    yu, yd, xu, xd = call(
        bind(near_kernel), "video_near", [f32(264, 768), block, block, block],
        *vectors, k2, ah, al, yl, yr, xl, xr, pos=pos, scratch=SCALES, flops=1024 * flops,
    )
    mine, yu = lax.optimization_barrier((mine, yu))
    far, up, down, own = call(audio_sum_kernel, "audio_sum", [f32(128, 768)] * 4, mine, got, pos=pos)
    far, yu, yd, xu, xd = lax.optimization_barrier((far, yu, yd, xu, xd))
    far = step_z(far, 1)
    yu, yd, xu, xd = step_y(yu, 1), step_y(yd, -1), step_x(xu, 1), step_x(xd, -1)
    y_own, x_own = call(
        bind(own_kernel), "video_own", [block, block], *vectors, k1, ah, al, pos=pos,
        scratch=SCALES, flops=512 * flops,
    )
    (up,) = call(add_kernel, "audio_add", [f32(128, 768)], up, far, mib=8)
    up, y_own = lax.optimization_barrier((up, y_own))
    up, down = step_z(up, 1), step_z(down, -1)
    order = pltpu.VMEM((32, 128), F32)
    y1, y2, y3, y0, x1, x2, x3, x0 = call(
        middle_kernel, "video_middle", [f32(72, 768)] * 4 + [f32(64, 768)] * 4,
        tpart, yl, yr, y_own, x_own, yu, yd, xu, xd, pos=pos, scratch=[pltpu.VMEM((256, 768), F32), order],
    )
    y1, y2, y3 = step_x(y1, 1), step_x(y2, 2), step_x(y3, 3)
    x1, x2, x3 = step_y(x1, 1), step_y(x2, 2), step_y(x3, 3)
    (audio_grad,) = call(audio_project_kernel, "audio_grad", [f32(128, 768)], audio, own, up, down)
    video_grad, loss = call(
        bind(video_kernel), "video_grad", [f32(128, 768), f32(1, 1)],
        video, y0, y1, y2, y3, x0, x1, x2, x3, pos=pos, scratch=[order],
    )
    return (loss[0, 0], audio_grad, video_grad)


def solution(mesh):
    in_specs = (P(("row", "col"), None), P(("col", "row"), None))
    out_specs = (P(), P(("row", "col"), None), P(("col", "row"), None))
    return jax.shard_map(local, mesh=mesh, in_specs=in_specs, out_specs=out_specs, check_vma=False)
```

```python
import jax
import jax.numpy as jnp
from jax import lax
from jax.experimental import pallas as pl
from jax.experimental.pallas import tpu as pltpu
from jax.sharding import PartitionSpec as P

ITERS = 3
F32 = jnp.float32
BF16 = jnp.bfloat16
MIB = 1024 * 1024
NEAR = (0, -1, 1, 2)


def vmem():
    return pl.BlockSpec(memory_space=pltpu.VMEM)


def smem():
    return pl.BlockSpec(memory_space=pltpu.SMEM)


def f32(*shape):
    return jax.ShapeDtypeStruct(shape, F32)


def bf16(*shape):
    return jax.ShapeDtypeStruct(shape, BF16)


def call(kernel, name, outs, *args, pos=None, scratch=(), mib=20, flops=0, light=False):
    specs = [vmem()] * len(args)
    if pos is not None:
        specs, args = [smem()] + specs, (pos,) + args
    size = lambda arrays: sum(a.size * a.dtype.itemsize for a in arrays)
    cost = pl.CostEstimate(
        flops=0 if light else flops,
        bytes_accessed=0 if light else size(args) + size(outs),
        transcendentals=0,
    )
    return pl.pallas_call(
        kernel,
        out_shape=list(outs),
        in_specs=specs,
        out_specs=[vmem()] * len(outs),
        scratch_shapes=list(scratch),
        compiler_params=pltpu.CompilerParams(vmem_limit_bytes=mib * MIB),
        cost_estimate=cost,
        name=name,
    )(*args)


def split(value):
    high = value.astype(BF16)
    return high, (value - high.astype(F32)).astype(BF16)


def dot3(lhs, rhs, dims):
    (lh, ll), (rh, rl) = lhs, rhs
    dot = lambda p, q: lax.dot_general(p, q, (dims, ((), ())), preferred_element_type=F32)
    return dot(lh, rh) + (dot(lh, rl) + dot(ll, rh))


def inverse_length(x):
    return lax.rsqrt(jnp.sum(x * x, axis=1, keepdims=True) + 1e-06)


def unit_kernel(a_ref, v_ref, au_ref, vt_ref, vb_ref):
    a = a_ref[...]
    au_ref[...] = a * inverse_length(a)
    v = v_ref[...]
    v = v * inverse_length(v)
    vt_ref[...] = v[:64]
    vb_ref[...] = v[64:]


LAYOUT = (
    ((0, 0), (1, 0)),
    ((0, 1), (0, 2), (1, 1), (1, 2)),
    ((0, 3), (1, 3)),
)


def join_kernel(axis, pos_ref, own, left, right, far, out_ref):
    size = own.shape[0]
    for j, ref in enumerate((own, left, right, far)):
        at = ((pos_ref[axis] + NEAR[j] + 4) % 4) * size
        out_ref[pl.ds(pl.multiple_of(at, size), size), :] = ref[...]


def halves_kernel(left, right, a_ref, b_ref):
    a_ref[...] = left[0:128, :]
    b_ref[...] = right[128:256, :]


def pieces_body(total, pieces, ah_ref, al_ref, k_ref, vh_ref, vl_ref):
    at = 0
    for piece in pieces:
        rows = slice(at, at + piece.shape[0])
        vh_ref[rows, :], vl_ref[rows, :] = split(piece[...])
        at += piece.shape[0]
        if at % 256 == 0:
            rows = slice(at - 256, at)
            video = (vh_ref[rows, :], vl_ref[rows, :])
            k = jnp.exp(20.0 * dot3(video, (ah_ref[...], al_ref[...]), ((1,), (1,))))
            k_ref[rows, :] = k
            total = total + jnp.sum(k.reshape(-1, 8, k.shape[1]), axis=0)
    return total


def scores_own_kernel(a_ref, b_ref, p_ref, q_ref, ah_ref, al_ref, k_ref, vh_ref, vl_ref, sum_ref):
    ah_ref[0:512, :], al_ref[0:512, :] = split(a_ref[...])
    ah_ref[512:1024, :], al_ref[512:1024, :] = split(b_ref[...])
    sum_ref[...] = pieces_body(0.0, (p_ref, q_ref), ah_ref, al_ref, k_ref, vh_ref, vl_ref)


def scores_near_kernel(ah_ref, al_ref, in_ref, p0, p1, p2, p3, k_ref, vh_ref, vl_ref, sum_ref):
    sum_ref[...] = pieces_body(in_ref[...], (p0, p1, p2, p3), ah_ref, al_ref, k_ref, vh_ref, vl_ref)


def scores_far_kernel(pos_ref, ah_ref, al_ref, in_ref, p0, p1, q0, q1, k_ref, vh_ref, vl_ref, sum_ref):
    total = pieces_body(in_ref[...], (p0, p1, q0, q1), ah_ref, al_ref, k_ref, vh_ref, vl_ref)
    put_lanes(pos_ref, sum_ref, jnp.sum(total, axis=0, keepdims=True))


def put_lanes(pos_ref, ref, row):
    for d in range(8):
        swapped = 4 * ((pos_ref[3] + d) % 2)
        for m in range(8):
            ref[d, pl.ds((m + swapped) % 8, 1), :] = row[:, m * 128 : m * 128 + 128]


def scale_of(part_ref):
    return 1.0 / jnp.sum(part_ref[...], axis=0)


def chunk_of(pos_ref, half, j, b):
    return half * 8 + ((pos_ref[half] + NEAR[j] + 4) % 4) * 2 + b


def chunks(pos_ref, k_refs):
    for ref, blocks in zip(k_refs, LAYOUT):
        for n, (half, j) in enumerate(blocks):
            for b in range(2):
                yield ref, n * 256 + b * 128, chunk_of(pos_ref, half, j, b)


def down(scale_ref, chunk):
    return jnp.broadcast_to(scale_ref[pl.ds(chunk, 1), :], (128, 128)).T


def columns_kernel(pos_ref, part_ref, k1_ref, k2_ref, k3_ref, out_ref):
    r = scale_of(part_ref)
    for ref, at, chunk in chunks(pos_ref, (k1_ref, k2_ref, k3_ref)):
        acc = ref[at : at + 128, 0:128] * r[0:1, :]
        for m in range(1, 8):
            acc = acc + ref[at : at + 128, m * 128 : m * 128 + 128] * r[m : m + 1, :]
        row = jnp.sum(acc.T, axis=0, keepdims=True)
        for d in range(16):
            out_ref[d, pl.ds(chunk, 1), :] = row


def fold(value):
    return jnp.sum(value.reshape(16, 8, 128), axis=0)


def rows_kernel(pos_ref, part_ref, k1_ref, k2_ref, k3_ref, out_ref, scale_ref):
    scale_ref[...] = scale_of(part_ref)
    acc = [0.0] * 8
    for ref, at, chunk in chunks(pos_ref, (k1_ref, k2_ref, k3_ref)):
        c = down(scale_ref, chunk)
        for m in range(8):
            acc[m] = acc[m] + fold(ref[at : at + 128, m * 128 : m * 128 + 128] * c)
    put_lanes(pos_ref, out_ref, jnp.concatenate([jnp.sum(a, axis=0, keepdims=True) for a in acc], axis=1))


def last_rows_kernel(pos_ref, part_ref, rpart_ref, tot_ref, k1_ref, k2_ref, k3_ref, out_ref, scale_ref):
    scale_ref[...] = scale_of(part_ref)
    acc, weighted = [0.0] * 8, [0.0] * 8
    for ref, at, chunk in chunks(pos_ref, (k1_ref, k2_ref, k3_ref)):
        c = down(scale_ref, chunk)
        for m in range(8):
            kernel = ref[at : at + 128, m * 128 : m * 128 + 128]
            prod = kernel * c
            acc[m] = acc[m] + fold(prod)
            weighted[m] = weighted[m] + fold(prod * jnp.log(kernel))
    r = scale_of(rpart_ref)
    logs = jnp.log(jnp.sum(tot_ref[...], axis=0))
    terms = sum(r[m : m + 1] * (weighted[m] - logs[m : m + 1] * acc[m]) for m in range(8))
    put_lanes(pos_ref, out_ref, jnp.concatenate([jnp.sum(a, axis=0, keepdims=True) for a in acc], axis=1))
    for d in range(8):
        out_ref[d, 8:16, :] = terms


def grad_scales(count, tot_ref, rp_ref, cp_ref, tp_ref, c_ref, r_ref, w_ref):
    c_ref[...] = scale_of(cp_ref)
    r = scale_of(rp_ref) * (20.0 / count)
    w = r * jnp.sum(tp_ref[:, 0:8, :], axis=0) / jnp.sum(tot_ref[...], axis=0)
    for m in range(8):
        lanes = slice(m * 128, m * 128 + 128)
        r_ref[:, lanes] = jnp.broadcast_to(r[m : m + 1], (8, 128))
        w_ref[:, lanes] = jnp.broadcast_to(w[m : m + 1], (8, 128))


def grad_block(pos_ref, half, j, k_ref, at, c_ref, r_ref, w_ref):
    c = jnp.concatenate([down(c_ref, chunk_of(pos_ref, half, j, b)) for b in range(2)], axis=0)
    c = jnp.concatenate([c] * 8, axis=1)
    return split(k_ref[at : at + 256, :] * (w_ref[0:1, :] - r_ref[0:1, :] * c))


SCALES = [pltpu.VMEM((16, 128), F32), pltpu.VMEM((8, 1024), F32), pltpu.VMEM((8, 1024), F32)]


def far_kernel(count, pos_ref, tot_ref, rp_ref, cp_ref, tp_ref, k_ref, ah_ref, al_ref,
               yu_ref, yd_ref, xu_ref, xd_ref, c_ref, r_ref, w_ref):
    grad_scales(count, tot_ref, rp_ref, cp_ref, tp_ref, c_ref, r_ref, w_ref)
    for half, (u_ref, d_ref) in enumerate(((yu_ref, yd_ref), (xu_ref, xd_ref))):
        g = grad_block(pos_ref, half, 3, k_ref, half * 256, c_ref, r_ref, w_ref)
        out = dot3(g, (ah_ref[...], al_ref[...]), ((1,), (0,)))
        u_ref[0:128, :] = out[:128]
        d_ref[0:128, :] = out[128:]
    terms = jnp.concatenate([jnp.sum(tp_ref[:, 8:16, :], axis=0)] * 6, axis=1)
    yu_ref[128:136, :] = terms
    yd_ref[128:136, :] = terms


def audio_body(pos_ref, layouts, start, u_ref, c_ref, r_ref, w_ref, outs):
    for k_ref, h_ref, l_ref, first, blocks in layouts:
        for n, (half, j) in enumerate(blocks, first):
            at = slice(n * 256, n * 256 + 256)
            g = grad_block(pos_ref, half, j, k_ref, n * 256, c_ref, r_ref, w_ref)
            for m in range(4):
                lanes = slice(m * 256, m * 256 + 256)
                part = tuple(v[:, lanes] for v in g)
                out = dot3(part, (h_ref[at, :], l_ref[at, :]), ((0,), (0,)))
                out = out if start is None else start[lanes, :] + out
                if k_ref is layouts[-1][0] and n == first + len(blocks) - 1:
                    outs[m // 2][m % 2 * 256 : m % 2 * 256 + 256, :] = out
                else:
                    u_ref[lanes, :] = out
            start = u_ref


def audio_kernel(count, pos_ref, tot_ref, rp_ref, cp_ref, tp_ref, k1_ref, k2_ref, k3_ref,
                 h1_ref, l1_ref, h2_ref, l2_ref, h3_ref, l3_ref, mine_ref, other_ref,
                 c_ref, r_ref, w_ref, u_ref):
    grad_scales(count, tot_ref, rp_ref, cp_ref, tp_ref, c_ref, r_ref, w_ref)
    layouts = (
        (k1_ref, h1_ref, l1_ref, 0, LAYOUT[0]),
        (k3_ref, h3_ref, l3_ref, 0, LAYOUT[2]),
        (k2_ref, h2_ref, l2_ref, 0, LAYOUT[1]),
    )
    audio_body(pos_ref, layouts, None, u_ref, c_ref, r_ref, w_ref, (mine_ref, other_ref))


def near_kernel(count, pos_ref, tot_ref, rp_ref, cp_ref, tp_ref, k_ref, ah_ref, al_ref,
                yl_ref, yr_ref, xl_ref, xr_ref, yu_ref, yd_ref, xu_ref, xd_ref, c_ref, r_ref, w_ref):
    grad_scales(count, tot_ref, rp_ref, cp_ref, tp_ref, c_ref, r_ref, w_ref)
    for n, (ref, left, right) in enumerate((
        (yd_ref, None, yr_ref), (yu_ref, yl_ref, None), (xd_ref, None, xr_ref), (xu_ref, xl_ref, None)
    )):
        half, j = LAYOUT[1][n]
        g = grad_block(pos_ref, half, j, k_ref, n * 256, c_ref, r_ref, w_ref)
        out = dot3(g, (ah_ref[...], al_ref[...]), ((1,), (0,)))
        ref[0:128, :] = out[:128] if left is None else out[:128] + left[0:128, :]
        ref[128:256, :] = out[128:] if right is None else out[128:] + right[0:128, :]
    yu_ref[256:264, :] = yl_ref[128:136, :]


def own_kernel(count, pos_ref, tot_ref, rp_ref, cp_ref, tp_ref, k_ref, ah_ref, al_ref,
               y_ref, x_ref, c_ref, r_ref, w_ref):
    grad_scales(count, tot_ref, rp_ref, cp_ref, tp_ref, c_ref, r_ref, w_ref)
    for half, ref in enumerate((y_ref, x_ref)):
        g = grad_block(pos_ref, half, 0, k_ref, half * 256, c_ref, r_ref, w_ref)
        ref[...] = dot3(g, (ah_ref[...], al_ref[...]), ((1,), (0,)))


def ordered_sum(me, values, order_ref):
    for k, value in enumerate(values):
        order_ref[pl.ds(pl.multiple_of(((me + k) % 4) * 8, 8), 8), :] = value
    return jnp.sum(order_ref[...].reshape(4, 8, 128), axis=0)


def middle_kernel(pos_ref, tp_ref, yl_ref, yr_ref, y_ref, x_ref, yu_ref, yd_ref, xu_ref, xd_ref,
                  y1_ref, y2_ref, y3_ref, y0_ref, x1_ref, x2_ref, x3_ref, x0_ref, sum_ref, order_ref):
    terms = ordered_sum(
        pos_ref[0],
        (jnp.sum(tp_ref[:, 8:16, :], axis=0), yr_ref[128:136, 0:128], yu_ref[256:264, 0:128],
         yl_ref[128:136, 0:128]),
        order_ref,
    )
    for half, (own, up, down, outs) in enumerate((
        (y_ref, yu_ref, yd_ref, (y0_ref, y1_ref, y2_ref, y3_ref)),
        (x_ref, xu_ref, xd_ref, (x0_ref, x1_ref, x2_ref, x3_ref)),
    )):
        sum_ref[...] = own[...] + up[0:256, :] + down[...]
        for k, ref in enumerate(outs):
            at = ((pos_ref[1 - half] + k) % 4) * 64
            ref[0:64, :] = sum_ref[pl.ds(pl.multiple_of(at, 64), 64), :]
            if half == 0:
                ref[64:72, :] = jnp.concatenate([terms] * 6, axis=1)


def audio_sum_kernel(pos_ref, mine_ref, got_ref, far_ref, up_ref, down_ref, own_ref):
    for k, ref in ((2, far_ref), (1, up_ref), (3, down_ref), (0, own_ref)):
        at = pl.ds(pl.multiple_of(((pos_ref[2] + k) % 4) * 128, 128), 128)
        ref[...] = mine_ref[at, :] + got_ref[at, :]


def add_kernel(a_ref, b_ref, out_ref):
    out_ref[...] = a_ref[...] + b_ref[...]


def project(x, grad):
    inv = inverse_length(x)
    unit = x * inv
    return (grad - unit * jnp.sum(unit * grad, axis=1, keepdims=True)) * inv


def video_kernel(count, pos_ref, v_ref, y0, y1, y2, y3, x0, x1, x2, x3, out_ref, loss_ref, order_ref):
    top = y0[0:64, :] + y1[0:64, :] + y2[0:64, :] + y3[0:64, :]
    bottom = x0[...] + x1[...] + x2[...] + x3[...]
    out_ref[0:64, :] = project(v_ref[0:64, :], top)
    out_ref[64:128, :] = project(v_ref[64:128, :], bottom)
    terms = ordered_sum(
        pos_ref[1], tuple(ref[64:72, 0:128] for ref in (y0, y3, y2, y1)), order_ref
    )
    loss_ref[...] = jnp.full((1, 1), -jnp.sum(terms) / count)


def audio_project_kernel(x_ref, own_ref, up_ref, down_ref, out_ref):
    out_ref[...] = project(x_ref[...], own_ref[...] + up_ref[...] + down_ref[...])


def step_y(v, k):
    return lax.ppermute(v, "row", [(i, ((i // 4 + k) % 4) * 4 + i % 4) for i in range(16)])


def step_x(v, k):
    return lax.ppermute(v, "row", [(i, (i // 4) * 4 + (i % 4 + k) % 4) for i in range(16)])


def step_z(v, k):
    return lax.ppermute(v, "col", [(i, ((i // 2 + k) % 4) * 2 + i % 2) for i in range(8)])


def other_core(v):
    return lax.ppermute(v, "col", [(i, i ^ 1) for i in range(8)])


def swap(part, axis):
    return lax.all_to_all(part, axis, 0, 0, tiled=True)


def local(audio, video):
    count = audio.shape[0] * 128
    bind = lambda kernel: lambda *refs: kernel(count, *refs)
    row = lax.axis_index("row")
    col = lax.axis_index("col")
    pos = jnp.stack([row // 4, row % 4, col // 2, col % 2]).astype(jnp.int32)
    audio_unit, vt, vb = call(
        unit_kernel, "unit_rows", [f32(128, 768), f32(64, 768), f32(64, 768)],
        *(pltpu.with_memory_space_constraint(a, pltpu.HBM) for a in (audio, video)),
    )
    join = lambda axis, *parts: call(
        lambda *refs: join_kernel(axis, *refs), "join", [f32(4 * parts[0].shape[0], 768)], *parts, pos=pos, mib=8
    )[0]
    xl, xr, yl, yr = step_x(vt, 1), step_x(vt, -1), step_y(vb, 1), step_y(vb, -1)
    zl, zr = step_z(audio_unit, 1), step_z(audio_unit, -1)
    yr, xl, xr = lax.optimization_barrier((yr, xl, xr))
    first = join(1, vt, xl, xr, step_x(xl, 1))
    second = join(0, vb, yl, yr, step_y(yr, -1))
    zl, _, _ = lax.optimization_barrier((zl, first, second))
    fl, fr, sl, sr = step_y(first, 1), step_y(first, -1), step_x(second, 1), step_x(second, -1)
    zf = lax.optimization_barrier((step_z(zl, 1), fl, fr, sl, sr))[0]
    audio_own = join(2, audio_unit, zl, zr, zf)
    audio_other = other_core(audio_own)
    flops = 3 * 2 * 1024 * 768
    ah, al, k1, h1, l1, sums = call(
        scores_own_kernel, "scores_own",
        [bf16(1024, 768), bf16(1024, 768), f32(512, 1024), bf16(512, 768), bf16(512, 768), f32(8, 1024)],
        audio_own, audio_other, first, second, light=True,
    )
    halves = lambda left, right: call(halves_kernel, "halves", [f32(128, 768)] * 2, left, right, mib=8)
    c, d = halves(sl, sr)
    fl, fr, c = lax.optimization_barrier((fl, fr, c))
    a, b = halves(fl, fr)
    far = (step_y(a, 1), step_y(b, -1), step_x(c, 1), step_x(d, -1))
    k2, h2, l2, sums = call(
        scores_near_kernel, "scores_near",
        [f32(1024, 1024), bf16(1024, 768), bf16(1024, 768), f32(8, 1024)],
        ah, al, sums, fl, fr, sl, sr, light=True,
    )
    k3, h3, l3, part = call(
        scores_far_kernel, "scores_far",
        [f32(512, 1024), bf16(512, 768), bf16(512, 768), f32(8, 8, 128)],
        ah, al, sums, *far, pos=pos, light=True,
    )
    ks = (k1, k2, k3)
    scale = pltpu.VMEM((16, 128), F32)
    totals = swap(part, "col")
    rpart = totals
    for step in range(ITERS):
        cpart = swap(call(columns_kernel, "column_sums", [f32(16, 16, 128)], rpart, *ks, pos=pos, mib=14)[0], "row")
        if step < ITERS - 1:
            part = call(rows_kernel, "row_sums", [f32(8, 8, 128)], cpart, *ks, pos=pos, mib=14, scratch=[scale])[0]
            rpart = swap(part, "col")
    part = call(last_rows_kernel, "row_sums_and_loss", [f32(8, 16, 128)], cpart, rpart, totals, *ks,
                pos=pos, mib=14, scratch=[scale])[0]
    tpart = swap(part, "col")

    vectors = (totals, rpart, cpart, tpart)
    block = f32(256, 768)
    yu, yd, xu, xd = call(
        bind(far_kernel), "video_far", [f32(136, 768), f32(136, 768), f32(128, 768), f32(128, 768)],
        *vectors, k3, ah, al, pos=pos, scratch=SCALES, flops=512 * flops,
    )
    after, yu = lax.optimization_barrier((tpart, yu))
    yl, yr, xl, xr = step_y(yu, 1), step_y(yd, -1), step_x(xu, 1), step_x(xd, -1)
    mine, other = call(
        bind(audio_kernel), "audio_all", [f32(512, 768)] * 2, totals, rpart, cpart, after, *ks,
        h1, l1, h2, l2, h3, l3, pos=pos, scratch=SCALES + [pltpu.VMEM((1024, 768), F32)],
        flops=2048 * flops, mib=28,
    )
    yl, yr, xl, xr, mine, other = lax.optimization_barrier((yl, yr, xl, xr, mine, other))
    got = other_core(other)
    yu, yd, xu, xd = call(
        bind(near_kernel), "video_near", [f32(264, 768), block, block, block],
        *vectors, k2, ah, al, yl, yr, xl, xr, pos=pos, scratch=SCALES, flops=1024 * flops,
    )
    mine, yu = lax.optimization_barrier((mine, yu))
    far, up, down, own = call(audio_sum_kernel, "audio_sum", [f32(128, 768)] * 4, mine, got, pos=pos)
    far, yu, yd, xu, xd = lax.optimization_barrier((far, yu, yd, xu, xd))
    far = step_z(far, 1)
    yu, yd, xu, xd = step_y(yu, 1), step_y(yd, -1), step_x(xu, 1), step_x(xd, -1)
    y_own, x_own = call(
        bind(own_kernel), "video_own", [block, block], *vectors, k1, ah, al, pos=pos,
        scratch=SCALES, flops=512 * flops,
    )
    (up,) = call(add_kernel, "audio_add", [f32(128, 768)], up, far, mib=8)
    up, y_own = lax.optimization_barrier((up, y_own))
    up, down = step_z(up, 1), step_z(down, -1)
    order = pltpu.VMEM((32, 128), F32)
    y1, y2, y3, y0, x1, x2, x3, x0 = call(
        middle_kernel, "video_middle", [f32(72, 768)] * 4 + [f32(64, 768)] * 4,
        tpart, yl, yr, y_own, x_own, yu, yd, xu, xd, pos=pos, scratch=[pltpu.VMEM((256, 768), F32), order],
    )
    y1, y2, y3 = step_x(y1, 1), step_x(y2, 2), step_x(y3, 3)
    x1, x3, y1 = lax.optimization_barrier((x1, x3, y1))
    x1, x2, x3 = step_y(x1, 1), step_y(x2, 2), step_y(x3, 3)
    (audio_grad,) = call(audio_project_kernel, "audio_grad", [f32(128, 768)], audio, own, up, down)
    video_grad, loss = call(
        bind(video_kernel), "video_grad", [f32(128, 768), f32(1, 1)],
        video, y0, y1, y2, y3, x0, x1, x2, x3, pos=pos, scratch=[order],
    )
    return (loss[0, 0], audio_grad, video_grad)


def solution(mesh):
    in_specs = (P(("row", "col"), None), P(("col", "row"), None))
    out_specs = (P(), P(("row", "col"), None), P(("col", "row"), None))
    return jax.shard_map(local, mesh=mesh, in_specs=in_specs, out_specs=out_specs, check_vma=False)
```

```python
import jax
import jax.numpy as jnp
from jax import lax
from jax.experimental import pallas as pl
from jax.experimental.pallas import tpu as pltpu
from jax.sharding import PartitionSpec as P

ITERS = 3
F32 = jnp.float32
BF16 = jnp.bfloat16
MIB = 1024 * 1024
NEAR = (0, -1, 1, 2)


def vmem():
    return pl.BlockSpec(memory_space=pltpu.VMEM)


def smem():
    return pl.BlockSpec(memory_space=pltpu.SMEM)


def f32(*shape):
    return jax.ShapeDtypeStruct(shape, F32)


def bf16(*shape):
    return jax.ShapeDtypeStruct(shape, BF16)


def call(kernel, name, outs, *args, pos=None, scratch=(), mib=20, flops=0, light=False):
    specs = [vmem()] * len(args)
    if pos is not None:
        specs, args = [smem()] + specs, (pos,) + args
    size = lambda arrays: sum(a.size * a.dtype.itemsize for a in arrays)
    cost = pl.CostEstimate(
        flops=0 if light else flops,
        bytes_accessed=0 if light else size(args) + size(outs),
        transcendentals=0,
    )
    return pl.pallas_call(
        kernel,
        out_shape=list(outs),
        in_specs=specs,
        out_specs=[vmem()] * len(outs),
        scratch_shapes=list(scratch),
        compiler_params=pltpu.CompilerParams(vmem_limit_bytes=mib * MIB),
        cost_estimate=cost,
        name=name,
    )(*args)


def split(value):
    high = value.astype(BF16)
    return high, (value - high.astype(F32)).astype(BF16)


def dot3(lhs, rhs, dims):
    (lh, ll), (rh, rl) = lhs, rhs
    dot = lambda p, q: lax.dot_general(p, q, (dims, ((), ())), preferred_element_type=F32)
    return dot(lh, rh) + (dot(lh, rl) + dot(ll, rh))


def inverse_length(x):
    return lax.rsqrt(jnp.sum(x * x, axis=1, keepdims=True) + 1e-06)


def unit_kernel(a_ref, v_ref, au_ref, vt_ref, vb_ref):
    a = a_ref[...]
    au_ref[...] = a * inverse_length(a)
    v = v_ref[...]
    v = v * inverse_length(v)
    vt_ref[...] = v[:64]
    vb_ref[...] = v[64:]


LAYOUT = (
    ((0, 0), (1, 0)),
    ((0, 1), (0, 2), (1, 1), (1, 2)),
    ((0, 3), (1, 3)),
)


def join_kernel(axis, pos_ref, own, left, right, far, out_ref):
    size = own.shape[0]
    for j, ref in enumerate((own, left, right, far)):
        at = ((pos_ref[axis] + NEAR[j] + 4) % 4) * size
        out_ref[pl.ds(pl.multiple_of(at, size), size), :] = ref[...]


def halves_kernel(left, right, a_ref, b_ref):
    a_ref[...] = left[0:128, :]
    b_ref[...] = right[128:256, :]


def pieces_body(total, pieces, ah_ref, al_ref, k_ref, vh_ref, vl_ref):
    at = 0
    for piece in pieces:
        rows = slice(at, at + piece.shape[0])
        vh_ref[rows, :], vl_ref[rows, :] = split(piece[...])
        at += piece.shape[0]
        if at % 256 == 0:
            rows = slice(at - 256, at)
            video = (vh_ref[rows, :], vl_ref[rows, :])
            k = jnp.exp(20.0 * dot3(video, (ah_ref[...], al_ref[...]), ((1,), (1,))))
            k_ref[rows, :] = k
            total = total + jnp.sum(k.reshape(-1, 8, k.shape[1]), axis=0)
    return total


def scores_own_kernel(a_ref, b_ref, p_ref, q_ref, ah_ref, al_ref, k_ref, vh_ref, vl_ref, sum_ref):
    ah_ref[0:512, :], al_ref[0:512, :] = split(a_ref[...])
    ah_ref[512:1024, :], al_ref[512:1024, :] = split(b_ref[...])
    sum_ref[...] = pieces_body(0.0, (p_ref, q_ref), ah_ref, al_ref, k_ref, vh_ref, vl_ref)


def scores_near_kernel(ah_ref, al_ref, in_ref, p0, p1, p2, p3, k_ref, vh_ref, vl_ref, sum_ref):
    sum_ref[...] = pieces_body(in_ref[...], (p0, p1, p2, p3), ah_ref, al_ref, k_ref, vh_ref, vl_ref)


def scores_far_kernel(pos_ref, ah_ref, al_ref, in_ref, p0, p1, q0, q1, k_ref, vh_ref, vl_ref, sum_ref):
    total = pieces_body(in_ref[...], (p0, p1, q0, q1), ah_ref, al_ref, k_ref, vh_ref, vl_ref)
    put_lanes(pos_ref, sum_ref, jnp.sum(total, axis=0, keepdims=True))


def put_lanes(pos_ref, ref, row):
    for d in range(2):
        swapped = 4 * ((pos_ref[3] + d) % 2)
        for m in range(8):
            ref[d, pl.ds((m + swapped) % 8, 1), :] = row[:, m * 128 : m * 128 + 128]
    for d in range(2, 8):
        ref[d, 0:8, :] = ref[d % 2, 0:8, :]


def scale_of(part_ref):
    return 1.0 / jnp.sum(part_ref[...], axis=0)


def chunk_of(pos_ref, half, j, b):
    return half * 8 + ((pos_ref[half] + NEAR[j] + 4) % 4) * 2 + b


def chunks(pos_ref, k_refs):
    for ref, blocks in zip(k_refs, LAYOUT):
        for n, (half, j) in enumerate(blocks):
            for b in range(2):
                yield ref, n * 256 + b * 128, chunk_of(pos_ref, half, j, b)


def down(scale_ref, chunk):
    return jnp.broadcast_to(scale_ref[pl.ds(chunk, 1), :], (128, 128)).T


def columns_kernel(pos_ref, part_ref, k1_ref, k2_ref, k3_ref, out_ref):
    r = scale_of(part_ref)
    for ref, at, chunk in chunks(pos_ref, (k1_ref, k2_ref, k3_ref)):
        acc = ref[at : at + 128, 0:128] * r[0:1, :]
        for m in range(1, 8):
            acc = acc + ref[at : at + 128, m * 128 : m * 128 + 128] * r[m : m + 1, :]
        out_ref[0, pl.ds(chunk, 1), :] = jnp.sum(acc.T, axis=0, keepdims=True)
    for d in range(1, 16):
        out_ref[d] = out_ref[0]


def fold(value):
    return jnp.sum(value.reshape(16, 8, 128), axis=0)


def rows_kernel(pos_ref, part_ref, k1_ref, k2_ref, k3_ref, out_ref, scale_ref):
    scale_ref[...] = scale_of(part_ref)
    acc = [0.0] * 8
    for ref, at, chunk in chunks(pos_ref, (k1_ref, k2_ref, k3_ref)):
        c = down(scale_ref, chunk)
        for m in range(8):
            acc[m] = acc[m] + fold(ref[at : at + 128, m * 128 : m * 128 + 128] * c)
    put_lanes(pos_ref, out_ref, jnp.concatenate([jnp.sum(a, axis=0, keepdims=True) for a in acc], axis=1))


def last_rows_kernel(pos_ref, part_ref, rpart_ref, tot_ref, k1_ref, k2_ref, k3_ref, out_ref, scale_ref):
    scale_ref[...] = scale_of(part_ref)
    acc, weighted = [0.0] * 8, [0.0] * 8
    for ref, at, chunk in chunks(pos_ref, (k1_ref, k2_ref, k3_ref)):
        c = down(scale_ref, chunk)
        for m in range(8):
            kernel = ref[at : at + 128, m * 128 : m * 128 + 128]
            prod = kernel * c
            acc[m] = acc[m] + fold(prod)
            weighted[m] = weighted[m] + fold(prod * jnp.log(kernel))
    r = scale_of(rpart_ref)
    logs = jnp.log(jnp.sum(tot_ref[...], axis=0))
    terms = sum(r[m : m + 1] * (weighted[m] - logs[m : m + 1] * acc[m]) for m in range(8))
    put_lanes(pos_ref, out_ref, jnp.concatenate([jnp.sum(a, axis=0, keepdims=True) for a in acc], axis=1))
    for d in range(8):
        out_ref[d, 8:16, :] = terms


def grad_scales(count, tot_ref, rp_ref, cp_ref, tp_ref, c_ref, r_ref, w_ref):
    c_ref[...] = scale_of(cp_ref)
    r = scale_of(rp_ref) * (20.0 / count)
    w = r * jnp.sum(tp_ref[:, 0:8, :], axis=0) / jnp.sum(tot_ref[...], axis=0)
    for m in range(8):
        lanes = slice(m * 128, m * 128 + 128)
        r_ref[:, lanes] = jnp.broadcast_to(r[m : m + 1], (8, 128))
        w_ref[:, lanes] = jnp.broadcast_to(w[m : m + 1], (8, 128))


def grad_block(pos_ref, half, j, k_ref, at, c_ref, r_ref, w_ref):
    c = jnp.concatenate([down(c_ref, chunk_of(pos_ref, half, j, b)) for b in range(2)], axis=0)
    c = jnp.concatenate([c] * 8, axis=1)
    return split(k_ref[at : at + 256, :] * (w_ref[0:1, :] - r_ref[0:1, :] * c))


SCALES = [pltpu.VMEM((16, 128), F32), pltpu.VMEM((8, 1024), F32), pltpu.VMEM((8, 1024), F32)]


def far_kernel(count, pos_ref, tot_ref, rp_ref, cp_ref, tp_ref, k_ref, ah_ref, al_ref,
               yu_ref, yd_ref, xu_ref, xd_ref, c_ref, r_ref, w_ref):
    grad_scales(count, tot_ref, rp_ref, cp_ref, tp_ref, c_ref, r_ref, w_ref)
    for half, (u_ref, d_ref) in enumerate(((yu_ref, yd_ref), (xu_ref, xd_ref))):
        g = grad_block(pos_ref, half, 3, k_ref, half * 256, c_ref, r_ref, w_ref)
        out = dot3(g, (ah_ref[...], al_ref[...]), ((1,), (0,)))
        u_ref[0:128, :] = out[:128]
        d_ref[0:128, :] = out[128:]
    terms = jnp.concatenate([jnp.sum(tp_ref[:, 8:16, :], axis=0)] * 6, axis=1)
    yu_ref[128:136, :] = terms
    yd_ref[128:136, :] = terms


def audio_body(pos_ref, layouts, start, u_ref, c_ref, r_ref, w_ref, outs):
    for k_ref, h_ref, l_ref, first, blocks in layouts:
        for n, (half, j) in enumerate(blocks, first):
            at = slice(n * 256, n * 256 + 256)
            g = grad_block(pos_ref, half, j, k_ref, n * 256, c_ref, r_ref, w_ref)
            for m in range(4):
                lanes = slice(m * 256, m * 256 + 256)
                part = tuple(v[:, lanes] for v in g)
                out = dot3(part, (h_ref[at, :], l_ref[at, :]), ((0,), (0,)))
                out = out if start is None else start[lanes, :] + out
                if k_ref is layouts[-1][0] and n == first + len(blocks) - 1:
                    outs[m // 2][m % 2 * 256 : m % 2 * 256 + 256, :] = out
                else:
                    u_ref[lanes, :] = out
            start = u_ref


def audio_kernel(count, pos_ref, tot_ref, rp_ref, cp_ref, tp_ref, k1_ref, k2_ref, k3_ref,
                 h1_ref, l1_ref, h2_ref, l2_ref, h3_ref, l3_ref, mine_ref, other_ref,
                 c_ref, r_ref, w_ref, u_ref):
    grad_scales(count, tot_ref, rp_ref, cp_ref, tp_ref, c_ref, r_ref, w_ref)
    layouts = (
        (k1_ref, h1_ref, l1_ref, 0, LAYOUT[0]),
        (k3_ref, h3_ref, l3_ref, 0, LAYOUT[2]),
        (k2_ref, h2_ref, l2_ref, 0, LAYOUT[1]),
    )
    audio_body(pos_ref, layouts, None, u_ref, c_ref, r_ref, w_ref, (mine_ref, other_ref))


def near_kernel(count, pos_ref, tot_ref, rp_ref, cp_ref, tp_ref, k_ref, ah_ref, al_ref,
                yl_ref, yr_ref, xl_ref, xr_ref, yu_ref, yd_ref, xu_ref, xd_ref, c_ref, r_ref, w_ref):
    grad_scales(count, tot_ref, rp_ref, cp_ref, tp_ref, c_ref, r_ref, w_ref)
    for n, (ref, left, right) in enumerate((
        (yd_ref, None, yr_ref), (yu_ref, yl_ref, None), (xd_ref, None, xr_ref), (xu_ref, xl_ref, None)
    )):
        half, j = LAYOUT[1][n]
        g = grad_block(pos_ref, half, j, k_ref, n * 256, c_ref, r_ref, w_ref)
        out = dot3(g, (ah_ref[...], al_ref[...]), ((1,), (0,)))
        ref[0:128, :] = out[:128] if left is None else out[:128] + left[0:128, :]
        ref[128:256, :] = out[128:] if right is None else out[128:] + right[0:128, :]
    yu_ref[256:264, :] = yl_ref[128:136, :]


def own_kernel(count, pos_ref, tot_ref, rp_ref, cp_ref, tp_ref, k_ref, ah_ref, al_ref,
               y_ref, x_ref, c_ref, r_ref, w_ref):
    grad_scales(count, tot_ref, rp_ref, cp_ref, tp_ref, c_ref, r_ref, w_ref)
    for half, ref in enumerate((y_ref, x_ref)):
        g = grad_block(pos_ref, half, 0, k_ref, half * 256, c_ref, r_ref, w_ref)
        ref[...] = dot3(g, (ah_ref[...], al_ref[...]), ((1,), (0,)))


def ordered_sum(me, values, order_ref):
    for k, value in enumerate(values):
        order_ref[pl.ds(pl.multiple_of(((me + k) % 4) * 8, 8), 8), :] = value
    return jnp.sum(order_ref[...].reshape(4, 8, 128), axis=0)


def middle_kernel(pos_ref, tp_ref, yl_ref, yr_ref, y_ref, x_ref, yu_ref, yd_ref, xu_ref, xd_ref,
                  y1_ref, y2_ref, y3_ref, y0_ref, x1_ref, x2_ref, x3_ref, x0_ref, sum_ref, order_ref):
    terms = ordered_sum(
        pos_ref[0],
        (jnp.sum(tp_ref[:, 8:16, :], axis=0), yr_ref[128:136, 0:128], yu_ref[256:264, 0:128],
         yl_ref[128:136, 0:128]),
        order_ref,
    )
    for half, (own, up, down, outs) in enumerate((
        (y_ref, yu_ref, yd_ref, (y0_ref, y1_ref, y2_ref, y3_ref)),
        (x_ref, xu_ref, xd_ref, (x0_ref, x1_ref, x2_ref, x3_ref)),
    )):
        sum_ref[...] = own[...] + up[0:256, :] + down[...]
        for k, ref in enumerate(outs):
            at = ((pos_ref[1 - half] + k) % 4) * 64
            ref[0:64, :] = sum_ref[pl.ds(pl.multiple_of(at, 64), 64), :]
            if half == 0:
                ref[64:72, :] = jnp.concatenate([terms] * 6, axis=1)


def audio_sum_kernel(pos_ref, mine_ref, got_ref, far_ref, up_ref, down_ref, own_ref):
    for k, ref in ((2, far_ref), (1, up_ref), (3, down_ref), (0, own_ref)):
        at = pl.ds(pl.multiple_of(((pos_ref[2] + k) % 4) * 128, 128), 128)
        ref[...] = mine_ref[at, :] + got_ref[at, :]


def add_kernel(a_ref, b_ref, out_ref):
    out_ref[...] = a_ref[...] + b_ref[...]


def project(x, grad):
    inv = inverse_length(x)
    unit = x * inv
    return (grad - unit * jnp.sum(unit * grad, axis=1, keepdims=True)) * inv


def video_kernel(count, pos_ref, v_ref, y0, y1, y2, y3, x0, x1, x2, x3, out_ref, loss_ref, order_ref):
    top = y0[0:64, :] + y1[0:64, :] + y2[0:64, :] + y3[0:64, :]
    bottom = x0[...] + x1[...] + x2[...] + x3[...]
    out_ref[0:64, :] = project(v_ref[0:64, :], top)
    out_ref[64:128, :] = project(v_ref[64:128, :], bottom)
    terms = ordered_sum(
        pos_ref[1], tuple(ref[64:72, 0:128] for ref in (y0, y3, y2, y1)), order_ref
    )
    loss_ref[...] = jnp.full((1, 1), -jnp.sum(terms) / count)


def audio_project_kernel(x_ref, own_ref, up_ref, down_ref, out_ref):
    out_ref[...] = project(x_ref[...], own_ref[...] + up_ref[...] + down_ref[...])


def step_y(v, k):
    return lax.ppermute(v, "row", [(i, ((i // 4 + k) % 4) * 4 + i % 4) for i in range(16)])


def step_x(v, k):
    return lax.ppermute(v, "row", [(i, (i // 4) * 4 + (i % 4 + k) % 4) for i in range(16)])


def step_z(v, k):
    return lax.ppermute(v, "col", [(i, ((i // 2 + k) % 4) * 2 + i % 2) for i in range(8)])


def other_core(v):
    return lax.ppermute(v, "col", [(i, i ^ 1) for i in range(8)])


def swap(part, axis):
    return lax.all_to_all(part, axis, 0, 0, tiled=True)


def local(audio, video):
    count = audio.shape[0] * 128
    bind = lambda kernel: lambda *refs: kernel(count, *refs)
    row = lax.axis_index("row")
    col = lax.axis_index("col")
    pos = jnp.stack([row // 4, row % 4, col // 2, col % 2]).astype(jnp.int32)
    audio_unit, vt, vb = call(
        unit_kernel, "unit_rows", [f32(128, 768), f32(64, 768), f32(64, 768)],
        *(pltpu.with_memory_space_constraint(a, pltpu.HBM) for a in (audio, video)),
    )
    join = lambda axis, *parts: call(
        lambda *refs: join_kernel(axis, *refs), "join", [f32(4 * parts[0].shape[0], 768)], *parts, pos=pos, mib=8
    )[0]
    xl, xr, yl, yr = step_x(vt, 1), step_x(vt, -1), step_y(vb, 1), step_y(vb, -1)
    zl, zr = step_z(audio_unit, 1), step_z(audio_unit, -1)
    yr, xl, xr = lax.optimization_barrier((yr, xl, xr))
    first = join(1, vt, xl, xr, step_x(xl, 1))
    second = join(0, vb, yl, yr, step_y(yr, -1))
    zl, _, _ = lax.optimization_barrier((zl, first, second))
    fl, fr, sl, sr = step_y(first, 1), step_y(first, -1), step_x(second, 1), step_x(second, -1)
    zf = lax.optimization_barrier((step_z(zl, 1), fl, fr, sl, sr))[0]
    audio_own = join(2, audio_unit, zl, zr, zf)
    audio_other = other_core(audio_own)
    flops = 3 * 2 * 1024 * 768
    ah, al, k1, h1, l1, sums = call(
        scores_own_kernel, "scores_own",
        [bf16(1024, 768), bf16(1024, 768), f32(512, 1024), bf16(512, 768), bf16(512, 768), f32(8, 1024)],
        audio_own, audio_other, first, second, light=True,
    )
    halves = lambda left, right: call(halves_kernel, "halves", [f32(128, 768)] * 2, left, right, mib=8)
    c, d = halves(sl, sr)
    fl, fr, c = lax.optimization_barrier((fl, fr, c))
    a, b = halves(fl, fr)
    far = (step_y(a, 1), step_y(b, -1), step_x(c, 1), step_x(d, -1))
    k2, h2, l2, sums = call(
        scores_near_kernel, "scores_near",
        [f32(1024, 1024), bf16(1024, 768), bf16(1024, 768), f32(8, 1024)],
        ah, al, sums, fl, fr, sl, sr, light=True,
    )
    k3, h3, l3, part = call(
        scores_far_kernel, "scores_far",
        [f32(512, 1024), bf16(512, 768), bf16(512, 768), f32(8, 8, 128)],
        ah, al, sums, *far, pos=pos, light=True,
    )
    ks = (k1, k2, k3)
    scale = pltpu.VMEM((16, 128), F32)
    totals = swap(part, "col")
    rpart = totals
    for step in range(ITERS):
        cpart = swap(call(columns_kernel, "column_sums", [f32(16, 16, 128)], rpart, *ks, pos=pos, mib=14)[0], "row")
        if step < ITERS - 1:
            part = call(rows_kernel, "row_sums", [f32(8, 8, 128)], cpart, *ks, pos=pos, mib=14, scratch=[scale])[0]
            rpart = swap(part, "col")
    part = call(last_rows_kernel, "row_sums_and_loss", [f32(8, 16, 128)], cpart, rpart, totals, *ks,
                pos=pos, mib=14, scratch=[scale])[0]
    tpart = swap(part, "col")

    vectors = (totals, rpart, cpart, tpart)
    block = f32(256, 768)
    yu, yd, xu, xd = call(
        bind(far_kernel), "video_far", [f32(136, 768), f32(136, 768), f32(128, 768), f32(128, 768)],
        *vectors, k3, ah, al, pos=pos, scratch=SCALES, flops=512 * flops,
    )
    after, yu = lax.optimization_barrier((tpart, yu))
    yl, yr, xl, xr = step_y(yu, 1), step_y(yd, -1), step_x(xu, 1), step_x(xd, -1)
    mine, other = call(
        bind(audio_kernel), "audio_all", [f32(512, 768)] * 2, totals, rpart, cpart, after, *ks,
        h1, l1, h2, l2, h3, l3, pos=pos, scratch=SCALES + [pltpu.VMEM((1024, 768), F32)],
        flops=2048 * flops, mib=28,
    )
    yl, yr, xl, xr, mine, other = lax.optimization_barrier((yl, yr, xl, xr, mine, other))
    got = other_core(other)
    yu, yd, xu, xd = call(
        bind(near_kernel), "video_near", [f32(264, 768), block, block, block],
        *vectors, k2, ah, al, yl, yr, xl, xr, pos=pos, scratch=SCALES, flops=1024 * flops,
    )
    mine, yu = lax.optimization_barrier((mine, yu))
    far, up, down, own = call(audio_sum_kernel, "audio_sum", [f32(128, 768)] * 4, mine, got, pos=pos)
    far, yu, yd, xu, xd = lax.optimization_barrier((far, yu, yd, xu, xd))
    far = step_z(far, 1)
    yu, yd, xu, xd = step_y(yu, 1), step_y(yd, -1), step_x(xu, 1), step_x(xd, -1)
    y_own, x_own = call(
        bind(own_kernel), "video_own", [block, block], *vectors, k1, ah, al, pos=pos,
        scratch=SCALES, flops=512 * flops,
    )
    (up,) = call(add_kernel, "audio_add", [f32(128, 768)], up, far, mib=8)
    up, y_own = lax.optimization_barrier((up, y_own))
    up, down = step_z(up, 1), step_z(down, -1)
    order = pltpu.VMEM((32, 128), F32)
    y1, y2, y3, y0, x1, x2, x3, x0 = call(
        middle_kernel, "video_middle", [f32(72, 768)] * 4 + [f32(64, 768)] * 4,
        tpart, yl, yr, y_own, x_own, yu, yd, xu, xd, pos=pos, scratch=[pltpu.VMEM((256, 768), F32), order],
    )
    y1, y2, y3 = step_x(y1, 1), step_x(y2, 2), step_x(y3, 3)
    x1, x3, y1 = lax.optimization_barrier((x1, x3, y1))
    x1, x2, x3 = step_y(x1, 1), step_y(x2, 2), step_y(x3, 3)
    (audio_grad,) = call(audio_project_kernel, "audio_grad", [f32(128, 768)], audio, own, up, down)
    video_grad, loss = call(
        bind(video_kernel), "video_grad", [f32(128, 768), f32(1, 1)],
        video, y0, y1, y2, y3, x0, x1, x2, x3, pos=pos, scratch=[order],
    )
    return (loss[0, 0], audio_grad, video_grad)


def solution(mesh):
    in_specs = (P(("row", "col"), None), P(("col", "row"), None))
    out_specs = (P(), P(("row", "col"), None), P(("col", "row"), None))
    return jax.shard_map(local, mesh=mesh, in_specs=in_specs, out_specs=out_specs, check_vma=False)
```
